256 devices in a mesh: dp: 32 (over z, x), mp: 8 (over y, core).
Axes of the slice: x: 4, y: 4, z: 8, core: 2. Of those that a mesh axis runs over, the one named last changes fastest.
Arguments:
- hidden: bfloat16 [4, 4096, 16384], P(None, 'dp', 'mp'), may hold values from -6 to 6
- queries: bfloat16 [4, 4096, 8192], P(None, 'dp', 'mp'), may hold values from -100 to 100
- rotated_token_keys: bfloat16 [4, 4096, 1024], P(None, 'dp', 'mp'), may hold values from -7 to 7
- stored_key_cache: bfloat16 [4096, 8, 64, 128], P('dp', 'mp'), may hold values from -6 to 6
- stored_value_cache: bfloat16 [4096, 8, 64, 128], P('dp', 'mp'), may hold values from -6 to 6
- row_cache_length: int32 [4096], P('dp'), may hold values from 1 to 64, as said below
- value_weight_matrix: bfloat16 [16384, 1024], P('mp'), may hold values from -0.0625 to 0.0625
- adapter_down_factor: float32 [64, 16384], P(None, 'mp'), may hold values from -0.046875 to 0.046875
- learner_down_gradient: bfloat16 [32, 64, 16384], P('dp', None, 'mp'), may hold values from -0.015625 to 0.015625
- adapter_up_factor: float32 [1024, 64], P('mp'), may hold values from -0.75 to 0.75
- learner_up_gradient: bfloat16 [32, 1024, 64], P('dp', 'mp'), may hold values from -0.25 to 0.25
Outputs:
- context: bfloat16 [4, 4096, 8192], P(None, 'dp', 'mp')
The draws below stay inside these ranges and needn't reach their ends.
Inputs may be any that keep to these rules, and one draw needn't show every extreme that they name: `row_cache_length`: some row has exactly 64 live positions in every draw; the 128 rows of each index of dp share one drawn ceiling, between 8 and 64.
All inputs are finite; a program needn't handle non-finite values.
Results may differ from the reference program's by a relative error of at most 0.0058.
Values sent between devices are 32-bit elements; how exact they have to be, the bound alone decides.
No kernel may reach another device: no remote copies, remote signals or barrier semaphores. Data moves between devices by JAX's collectives and lax.ppermute only.
A program may use at most 64 MiB of HBM per device.

```python
import jax
import jax.numpy as jnp
from jax import lax

MODEL_WIDTH = 16384
HD = 128
KVH = 8
GROUP = 8
ADAPTER_RANK = 64
STEPS = 4
CTX = 64
ROWS_DEV = 128
ROWS = 4096
VALUE_OUT_WIDTH = 1024
N_DP = 32


def draw_queries(key, part):
    key = jax.random.fold_in(key, 21)
    values = jnp.clip(jax.random.normal(key, (STEPS, ROWS, KVH, GROUP, HD), jnp.float32), -6.0, 6.0)
    return values.reshape(STEPS, ROWS, KVH * GROUP * HD).astype(jnp.bfloat16)


def draw_stored_key_cache(key, part):
    key = jax.random.fold_in(key, 22)
    values = jnp.clip(jax.random.normal(key, (ROWS, KVH, CTX, HD), jnp.float32), -6.0, 6.0)
    return values.astype(jnp.bfloat16)


def draw_rotated_token_keys(key, part):
    key = jax.random.fold_in(key, 23)
    values = jnp.clip(jax.random.normal(key, (STEPS, ROWS, KVH, HD), jnp.float32), -6.0, 6.0)
    return values.reshape(STEPS, ROWS, KVH * HD).astype(jnp.bfloat16)


def draw_row_cache_length(key, part):
    key = jax.random.fold_in(key, 5)
    key_caps, key_rows, key_pick = jax.random.split(key, 3)
    ceilings = jax.random.randint(key_caps, (N_DP, 1), max(CTX // 8, 1), CTX + 1)
    raw_draw = jax.random.randint(key_rows, (N_DP, ROWS_DEV), 0, 1 << 20)
    lengths = (1 + raw_draw % ceilings).reshape(ROWS)
    chosen = jax.random.randint(key_pick, (), 0, ROWS)
    return jnp.where(jnp.arange(ROWS) == chosen, CTX, lengths).astype(jnp.int32)


def spiked(drawn, key, source, target, blocks, factor):
    owner, partner = [(jnp.arange(drawn.shape[dim]) // (drawn.shape[dim] // blocks)).reshape([-1 if axis == dim else 1 for axis in range(drawn.ndim)]) for dim in (source, target)]
    chosen = jax.random.permutation(key, blocks)[partner]
    strong = (owner == chosen) | (owner == (partner + blocks // 2) % blocks)
    return jnp.where(strong, factor * drawn, drawn)


def steps_of(stream_key, shape, shards, least, largest):
    factor_of = 1.0
    for dim, shards_of in shards:
        steps = jax.random.uniform(jax.random.fold_in(jax.random.fold_in(stream_key, 6), dim), (shards_of,), jnp.float32, least / len(shards), largest / len(shards))
        factor_of = factor_of * jnp.repeat(jnp.exp(steps), shape[dim] // shards_of).reshape((-1,) + (1,) * (len(shape) - 1 - dim))
    return factor_of


def normal_values(key, dims, spread, reach, cuts=(), held_as=jnp.bfloat16):
    values = jax.random.normal(key, dims, jnp.float32) * spread
    if len(cuts) > 0:
        values = steps_of(key, dims, cuts, -0.22, 0.18) * values
    return jnp.clip(values, min=-reach, max=reach).astype(held_as)


def gaussian_with(stream_key, dims, width, bound, cuts, heavy, kind=jnp.bfloat16):
    drawn = width * jax.random.normal(stream_key, dims, jnp.float32)
    if cuts:
        drawn = drawn * steps_of(stream_key, dims, cuts, -0.22, 0.18)
    return jnp.clip(spiked(drawn, jax.random.fold_in(stream_key, 3), *heavy), -bound, bound).astype(kind)


def setup_inputs(seed: int = 0) -> dict:
    seeds = jax.random.split(jax.random.key(seed), 12)
    hidden = normal_values(seeds[0], (STEPS, ROWS, MODEL_WIDTH), 1.0, 6.0, ((1, 32), (2, 8)))
    queries = draw_queries(jax.random.fold_in(seeds[11], 71), 0)
    rotated_token_keys = draw_rotated_token_keys(jax.random.fold_in(seeds[11], 71), 0)
    stored_key_cache = draw_stored_key_cache(jax.random.fold_in(seeds[11], 71), 0)
    stored_value_cache = normal_values(seeds[4], (ROWS, KVH, CTX, HD), 1.0, 6.0, ((0, 32), (1, 8)))
    row_cache_length = draw_row_cache_length(jax.random.fold_in(seeds[11], 71), 0)
    value_weight_matrix = gaussian_with(seeds[6], (MODEL_WIDTH, VALUE_OUT_WIDTH), MODEL_WIDTH ** -0.5, 0.0625, ((0, 8),), (0, 1, 8, 2.0))
    adapter_down_factor = normal_values(seeds[7], (ADAPTER_RANK, MODEL_WIDTH), MODEL_WIDTH ** -0.5, 0.046875, ((1, 8),), jnp.float32)
    learner_down_gradient = normal_values(seeds[8], (N_DP, ADAPTER_RANK, MODEL_WIDTH), (MODEL_WIDTH * N_DP // 4) ** -0.5, 0.015625, ((0, 32), (2, 8)))
    adapter_up_factor = normal_values(seeds[9], (VALUE_OUT_WIDTH, ADAPTER_RANK), ADAPTER_RANK ** -0.5, 0.75, ((0, 8),), jnp.float32)
    learner_up_gradient = normal_values(seeds[10], (N_DP, VALUE_OUT_WIDTH, ADAPTER_RANK), (ADAPTER_RANK * N_DP // 4) ** -0.5, 0.25, ((0, 32), (1, 8)))
    return dict(hidden=hidden, queries=queries, rotated_token_keys=rotated_token_keys, stored_key_cache=stored_key_cache, stored_value_cache=stored_value_cache, row_cache_length=row_cache_length, value_weight_matrix=value_weight_matrix, adapter_down_factor=adapter_down_factor, learner_down_gradient=learner_down_gradient, adapter_up_factor=adapter_up_factor, learner_up_gradient=learner_up_gradient)


LEARNING_RATE = 0.5
ADAPTER_SCALE = 0.5

def reference(hidden, queries, rotated_token_keys, stored_key_cache, stored_value_cache, row_cache_length, value_weight_matrix, adapter_down_factor, learner_down_gradient, adapter_up_factor, learner_up_gradient):
    stepped_down_factor = adapter_down_factor - LEARNING_RATE * lax.optimization_barrier(jnp.sum(learner_down_gradient.astype(jnp.float32), axis=0))
    stepped_up_factor = adapter_up_factor - LEARNING_RATE * lax.optimization_barrier(jnp.sum(learner_up_gradient.astype(jnp.float32), axis=0))
    adapter_product = lax.dot_general(stepped_down_factor, stepped_up_factor, (((0,), (1,)), ((), ())), precision=lax.Precision.HIGHEST, preferred_element_type=jnp.float32)
    merged_value_weight = (value_weight_matrix.astype(jnp.float32) + ADAPTER_SCALE * adapter_product).astype(jnp.bfloat16)
    flat_hidden = hidden.reshape(STEPS * ROWS, MODEL_WIDTH)
    new_values = jnp.dot(flat_hidden, merged_value_weight, preferred_element_type=jnp.float32).astype(jnp.bfloat16)
    new_values = new_values.reshape(STEPS, ROWS, KVH, HD).transpose(2, 1, 0, 3)
    query_rows = queries.reshape(STEPS, ROWS, KVH, GROUP, HD).transpose(2, 1, 0, 3, 4).reshape(KVH, ROWS, STEPS * GROUP, HD)
    keys_new = rotated_token_keys.reshape(STEPS, ROWS, KVH, HD).transpose(2, 1, 0, 3)
    keys_cached = stored_key_cache.transpose(1, 0, 2, 3)
    values_cached = stored_value_cache.transpose(1, 0, 2, 3)
    live_mask = jnp.arange(CTX, dtype=jnp.int32)[None, :] < row_cache_length[:, None]
    causal = jnp.arange(STEPS, dtype=jnp.int32)[None, :] <= (jnp.arange(STEPS * GROUP, dtype=jnp.int32) // GROUP)[:, None]
    score_scale = 1.0 / jnp.sqrt(jnp.float32(HD))

    def one_head(pieces):
        query_head, key_head, value_head, cache_key_head, cache_value_head = pieces
        query_float = query_head.astype(jnp.float32)
        cache_scores = jnp.einsum('rqd,rkd->rqk', query_float, cache_key_head.astype(jnp.float32)) * score_scale
        fresh_scores = jnp.einsum('rqd,rud->rqu', query_float, key_head.astype(jnp.float32)) * score_scale
        cache_scores = jnp.where(live_mask[:, None, :], cache_scores, -jnp.inf)
        fresh_scores = jnp.where(causal[None], fresh_scores, -jnp.inf)
        row_max = jnp.maximum(lax.optimization_barrier(jnp.max(cache_scores, axis=-1)), lax.optimization_barrier(jnp.max(fresh_scores, axis=-1)))
        cache_exp = jnp.where(live_mask[:, None, :], jnp.exp(cache_scores - row_max[..., None]), 0.0)
        fresh_exp = jnp.where(causal[None], jnp.exp(fresh_scores - row_max[..., None]), 0.0)
        denominator = lax.optimization_barrier(jnp.sum(cache_exp, axis=-1)) + lax.optimization_barrier(jnp.sum(fresh_exp, axis=-1))
        cache_weights = (cache_exp / denominator[..., None]).astype(jnp.bfloat16)
        fresh_weights = (fresh_exp / denominator[..., None]).astype(jnp.bfloat16)
        summed = jnp.einsum('rqk,rkd->rqd', cache_weights.astype(jnp.float32), cache_value_head.astype(jnp.float32))
        summed = summed + jnp.einsum('rqu,rud->rqd', fresh_weights.astype(jnp.float32), value_head.astype(jnp.float32))
        return summed.astype(jnp.bfloat16)
    result = lax.map(one_head, (query_rows, keys_new, new_values, keys_cached, values_cached))
    return result.reshape(KVH, ROWS, STEPS, GROUP, HD).transpose(2, 1, 0, 3, 4).reshape(STEPS, ROWS, KVH * GROUP * HD)
```

```python
import functools

import jax
import jax.numpy as jnp
from jax import lax
from jax.experimental import pallas as pl
from jax.experimental.pallas import tpu as pltpu
from jax.sharding import PartitionSpec as P

LEARNING_RATE = 0.5
ADAPTER_SCALE = 0.5


def split_bf16(x):
    high = x.astype(jnp.bfloat16)
    low = (x - high.astype(jnp.float32)).astype(jnp.bfloat16)
    return high, low


def finish_kernel(heads, base_ref, u0, u1, u2, u3, b_ref, w_ref, cache_ref, out_ref, value_ref):
    t = pl.program_id(0)
    steps, rows, dim = value_ref.shape

    @pl.when(t == 0)
    def _():
        u = (u0[...] + u1[...]) + (u2[...] + u3[...])
        u_high, u_low = split_bf16(u)
        b_high, b_low = split_bf16(b_ref[...])
        dims = (((0,), (0,)), ((), ()))
        mm = functools.partial(
            lax.dot_general, dimension_numbers=dims, preferred_element_type=jnp.float32
        )
        delta = mm(b_high, u_high) + (mm(b_low, u_high) + mm(b_high, u_low))
        values = base_ref[...] + ADAPTER_SCALE * delta
        for s in range(steps):
            part = values[:, s * rows : (s + 1) * rows].T
            value_ref[s] = part.astype(jnp.bfloat16).astype(jnp.float32)

    for step in range(steps):

        @pl.when(t == step)
        def _():
            for g in range(heads):
                acc = cache_ref[0, :, g * dim : (g + 1) * dim]
                for s in range(step + 1):
                    j = (step * heads + g) * steps + s
                    acc = acc + w_ref[:, j : j + 1] * value_ref[s]
                out_ref[0, :, g * dim : (g + 1) * dim] = acc.astype(out_ref.dtype)


def shards(
    hidden,
    queries,
    rotated_token_keys,
    stored_key_cache,
    stored_value_cache,
    row_cache_length,
    value_weight_matrix,
    adapter_down_factor,
    learner_down_gradient,
    adapter_up_factor,
    learner_up_gradient,
):
    step_count, rows_dev, width_dev = hidden.shape
    heads_dev, ctx_len, head_dim = stored_key_cache.shape[1:]
    group_size = queries.shape[2] // (heads_dev * head_dim)
    rank = adapter_down_factor.shape[0]
    n_dp = lax.axis_size("dp")
    n_mp = lax.axis_size("mp")
    tokens = step_count * rows_dev
    flat_hidden = hidden.reshape(tokens, width_dev)

    term_a = -LEARNING_RATE * learner_down_gradient[0].astype(jnp.float32)
    term_b = -LEARNING_RATE * learner_up_gradient[0].astype(jnp.float32)
    terms = jnp.concatenate([term_a, term_b.T], axis=1)
    width = terms.shape[1]
    terms = terms.reshape(n_dp, rank // n_dp, width)
    mine = jnp.sum(lax.all_to_all(terms, "dp", 0, 0, tiled=True), axis=0)
    steps_ab = lax.all_to_all(
        jnp.broadcast_to(mine[None], terms.shape), "dp", 0, 0, tiled=True
    ).reshape(rank, width)
    new_a = adapter_down_factor + steps_ab[:, :width_dev]
    new_b = adapter_up_factor.T + steps_ab[:, width_dev:]

    base = lax.psum_scatter(
        lax.dot_general(
            value_weight_matrix,
            flat_hidden,
            (((0,), (1,)), ((), ())),
            preferred_element_type=jnp.float32,
        ),
        "mp",
        scatter_dimension=0,
        tiled=True,
    )

    a_split = jnp.concatenate(split_bf16(new_a), axis=0)
    inner = lax.dot_general(
        a_split, flat_hidden, (((1,), (1,)), ((), ())), preferred_element_type=jnp.float32
    )
    inner = inner[:rank] + inner[rank:]
    inner = inner + lax.ppermute(inner, "mp", [(i, i ^ 1) for i in range(n_mp)])
    inner_parts = [inner] + [
        lax.ppermute(inner, "mp", [(i, (i + 2 * k) % n_mp) for i in range(n_mp)])
        for k in range(1, n_mp // 2)
    ]

    query_rows = queries.reshape(step_count, rows_dev, group_size, head_dim).transpose(1, 0, 2, 3)
    query_rows = query_rows.reshape(rows_dev, step_count * group_size, head_dim)
    keys_new = rotated_token_keys.transpose(1, 0, 2)
    key_cache = stored_key_cache[:, 0]
    value_cache = stored_value_cache[:, 0]
    score_scale = 1.0 / jnp.sqrt(jnp.float32(head_dim))
    causal = (
        jnp.arange(step_count, dtype=jnp.int32)[None, :]
        <= (jnp.arange(step_count * group_size, dtype=jnp.int32) // group_size)[:, None]
    )
    fresh_scores = (
        jnp.einsum("rqd,rud->rqu", query_rows, keys_new, preferred_element_type=jnp.float32)
        * score_scale
    )
    fresh_scores = jnp.where(causal[None], fresh_scores, -jnp.inf)
    live_mask = jnp.arange(ctx_len, dtype=jnp.int32)[None, :] < row_cache_length[:, None]
    cache_scores = (
        jnp.einsum("rqd,rkd->rqk", query_rows, key_cache, preferred_element_type=jnp.float32)
        * score_scale
    )
    cache_scores = jnp.where(live_mask[:, None, :], cache_scores, -jnp.inf)
    row_max = jnp.maximum(jnp.max(cache_scores, axis=-1), jnp.max(fresh_scores, axis=-1))
    cache_exp = jnp.where(live_mask[:, None, :], jnp.exp(cache_scores - row_max[..., None]), 0.0)
    fresh_exp = jnp.where(causal[None], jnp.exp(fresh_scores - row_max[..., None]), 0.0)
    denominator = jnp.sum(cache_exp, axis=-1) + jnp.sum(fresh_exp, axis=-1)
    cache_weights = (cache_exp / denominator[..., None]).astype(jnp.bfloat16)
    fresh_weights = (fresh_exp / denominator[..., None]).astype(jnp.bfloat16)
    cache_part = jnp.einsum(
        "rqk,rkd->rqd", cache_weights, value_cache, preferred_element_type=jnp.float32
    )
    cache_part = (
        cache_part.reshape(rows_dev, step_count, group_size, head_dim)
        .transpose(1, 0, 2, 3)
        .reshape(step_count, rows_dev, group_size * head_dim)
    )
    fresh_flat = fresh_weights.astype(jnp.float32).reshape(
        rows_dev, step_count * group_size * step_count
    )

    whole = lambda a: pl.BlockSpec(a.shape, lambda t: (0,) * a.ndim)
    small = [base, *inner_parts, new_b, fresh_flat]
    step_spec = pl.BlockSpec((1, rows_dev, group_size * head_dim), lambda t: (t, 0, 0))
    return pl.pallas_call(
        functools.partial(finish_kernel, group_size),
        grid=(step_count,),
        out_shape=jax.ShapeDtypeStruct(queries.shape, jnp.bfloat16),
        in_specs=[whole(a) for a in small] + [step_spec],
        out_specs=step_spec,
        scratch_shapes=[pltpu.VMEM((step_count, rows_dev, head_dim), jnp.float32)],
        compiler_params=pltpu.CompilerParams(vmem_limit_bytes=16 * 1024 * 1024),
    )(*small, cache_part)


def solution(mesh):
    placed = (
        P(None, "dp", "mp"),
        P(None, "dp", "mp"),
        P(None, "dp", "mp"),
        P("dp", "mp", None, None),
        P("dp", "mp", None, None),
        P("dp"),
        P("mp", None),
        P(None, "mp"),
        P("dp", None, "mp"),
        P("mp", None),
        P("dp", "mp", None),
    )
    return jax.shard_map(
        shards, mesh=mesh, in_specs=placed, out_specs=P(None, "dp", "mp"), check_vma=False
    )
```

```python
import functools

import jax
import jax.numpy as jnp
from jax import lax
from jax.experimental import pallas as pl
from jax.experimental.pallas import tpu as pltpu
from jax.sharding import PartitionSpec as P

LEARNING_RATE = 0.5
ADAPTER_SCALE = 0.5


def split_bf16(x):
    high = x.astype(jnp.bfloat16)
    low = (x - high.astype(jnp.float32)).astype(jnp.bfloat16)
    return high, low


def project_kernel(place_ref, hidden_ref, weight_ref, keep_ref, send_ref):
    dim = keep_ref.shape[2]
    both = jnp.dot(hidden_ref[...], weight_ref[...], preferred_element_type=jnp.float32)
    first, second = both[:, :dim], both[:, dim:]
    odd = place_ref[1] == 1
    keep_ref[0] = jnp.where(odd, second, first)
    send_ref[0] = jnp.where(odd, first, second)


def terms_kernel(a_ref, b_ref, out_ref):
    width = a_ref.shape[1]
    slices, depth = out_ref.shape[:2]
    a = -LEARNING_RATE * a_ref[...].astype(jnp.float32)
    b = -LEARNING_RATE * b_ref[...].astype(jnp.float32)
    for i in range(slices):
        at = slice(i * depth, (i + 1) * depth)
        out_ref[i, :, :width] = a[at]
        out_ref[i, :, width:] = b[at]


def sum_kernel(in_ref, out_ref):
    total = jnp.sum(in_ref[...], axis=0, keepdims=True)
    out_ref[...] = jnp.broadcast_to(total, out_ref.shape)


def inner_kernel(a_ref, b_ref, step_ref, hidden_ref, inner_ref, new_b_ref, held_ref, sems):
    rank, width = a_ref.shape
    chunks, tokens, part = held_ref.shape
    copies = [
        pltpu.make_async_copy(
            hidden_ref.at[:, pl.ds(k * part, part)], held_ref.at[k], sems.at[k]
        )
        for k in range(chunks)
    ]
    for copy in copies:
        copy.start()
    steps = jnp.concatenate([step_ref[i] for i in range(step_ref.shape[0])], axis=0)
    new_b_ref[...] = b_ref[...] + steps[:, width:]
    new_a = a_ref[...] + steps[:, :width]
    parts = jnp.concatenate(split_bf16(new_a), axis=0)
    total = jnp.zeros((tokens, 2 * rank), jnp.float32)
    for k in range(chunks):
        copies[k].wait()
        total = total + lax.dot_general(
            held_ref[k],
            parts[:, k * part : (k + 1) * part],
            (((1,), (1,)), ((), ())),
            preferred_element_type=jnp.float32,
        )
    total = total.T
    inner_ref[...] = total[:rank] + total[rank:]


def cache_kernel(length_ref, query_ref, fresh_ref, key_ref, value_ref, part_ref, weight_ref, rows_ref):
    block = pl.program_id(0)
    steps, rows, width = query_ref.shape
    first = block * rows
    ctx, dim = key_ref.shape[1:]
    heads = width // dim
    n_queries = steps * heads
    scale = 1.0 / (dim**0.5)
    for t in range(steps):
        for g in range(heads):
            at = (t * heads + g) * rows
            rows_ref[at : at + rows] = query_ref[t, :, g * dim : (g + 1) * dim].astype(jnp.float32)

    @pl.when(block == 0)
    def _():
        weight_ref[...] = jnp.zeros_like(weight_ref)

    fresh_keys = fresh_ref[...].astype(jnp.bfloat16)
    lane = lax.broadcasted_iota(jnp.int32, (n_queries, 2 * ctx), 1)
    step_of = lax.broadcasted_iota(jnp.int32, (n_queries, 2 * ctx), 0) >> 3
    by_lane = (((1,), (1,)), ((), ()))
    mm = functools.partial(
        lax.dot_general, dimension_numbers=by_lane, preferred_element_type=jnp.float32
    )
    for r in range(0, rows, 2):
        pair = [rows_ref[pl.ds(r + h, n_queries, stride=rows), :] for h in (0, 1)]
        pair = jnp.concatenate(pair, axis=0).astype(jnp.bfloat16)
        cached = mm(pair, key_ref[r : r + 2].reshape(2 * ctx, dim)) * scale
        fresh = mm(pair, fresh_keys) * scale
        weights = []
        for h in (0, 1):
            part = slice(h * n_queries, (h + 1) * n_queries)
            live = (lane >= h * ctx) & (lane < h * ctx + length_ref[first + r + h])
            at = steps * (r + h)
            causal = (lane >= at) & (lane <= at + step_of)
            old = jnp.where(live, cached[part], -jnp.inf)
            new = jnp.where(causal, fresh[part], -jnp.inf)
            top = jnp.max(jnp.maximum(old, new), axis=1, keepdims=True)
            old, new = jnp.exp(old - top), jnp.exp(new - top)
            inverse = 1.0 / jnp.sum(old + new, axis=1, keepdims=True)
            weights.append((old * inverse).astype(jnp.bfloat16))
            new = (new * inverse).astype(jnp.bfloat16).astype(jnp.float32)
            new = pltpu.roll(new, lax.rem(2 * ctx - at + steps * block, 2 * ctx), 1)
            row = pl.ds(r + h, n_queries, stride=rows)
            weight_ref[row, :] = weight_ref[row, :] + new
        part = jnp.dot(
            jnp.concatenate(weights, axis=0),
            value_ref[r : r + 2].reshape(2 * ctx, dim),
            preferred_element_type=jnp.float32,
        )
        for h in (0, 1):
            part_ref[pl.ds(r + h, n_queries, stride=rows), :] = part[
                h * n_queries : (h + 1) * n_queries
            ]


def finish_kernel(base_ref, u0, u1, u2, u3, b_ref, w_ref, cache_ref, out_ref, value_ref):
    t = pl.program_id(0)
    steps, rows, dim = value_ref.shape
    blocks, heads, block_rows = cache_ref.shape[:3]

    @pl.when(t == 0)
    def _():
        u = (u0[...] + u1[...]) + (u2[...] + u3[...])
        u_high, u_low = split_bf16(u)
        b_high, b_low = split_bf16(b_ref[...])
        dims = (((0,), (0,)), ((), ()))
        mm = functools.partial(
            lax.dot_general, dimension_numbers=dims, preferred_element_type=jnp.float32
        )
        delta = mm(u_high, b_high) + (mm(u_low, b_high) + mm(u_high, b_low))
        values = base_ref[...] + ADAPTER_SCALE * delta
        values = values.astype(jnp.bfloat16).astype(jnp.float32)
        for s in range(steps):
            value_ref[s] = values[s * rows : (s + 1) * rows]

    for step in range(steps):

        @pl.when(t == step)
        def _():
            for g in range(heads):
                for i in range(blocks):
                    at = slice(i * block_rows, (i + 1) * block_rows)
                    acc = cache_ref[i, g]
                    weight = w_ref[g]
                    for s in range(step + 1):
                        lane = i * steps + s
                        acc = acc + weight[:, lane : lane + 1] * value_ref[s, at]
                    out_ref[0, at, g * dim : (g + 1) * dim] = acc.astype(out_ref.dtype)


def shards(
    hidden,
    queries,
    rotated_token_keys,
    stored_key_cache,
    stored_value_cache,
    row_cache_length,
    value_weight_matrix,
    adapter_down_factor,
    learner_down_gradient,
    adapter_up_factor,
    learner_up_gradient,
):
    step_count, rows_dev, width_dev = hidden.shape
    heads_dev, ctx_len, head_dim = stored_key_cache.shape[1:]
    group_size = queries.shape[2] // (heads_dev * head_dim)
    rank = adapter_down_factor.shape[0]
    n_dp = lax.axis_size("dp")
    n_mp = lax.axis_size("mp")
    tokens = step_count * rows_dev
    flat_hidden = hidden.reshape(tokens, width_dev)

    small_vmem = pltpu.CompilerParams(vmem_limit_bytes=16 * 1024 * 1024)

    slices = jax.ShapeDtypeStruct((n_dp, rank // n_dp, width_dev + head_dim), jnp.float32)
    terms = pl.pallas_call(terms_kernel, out_shape=slices, compiler_params=small_vmem)(
        learner_down_gradient[0], learner_up_gradient[0].T
    )
    mine = lax.all_to_all(terms, "dp", 0, 0, tiled=True)
    mine = pl.pallas_call(sum_kernel, out_shape=slices, compiler_params=small_vmem)(mine)

    n_chips = n_mp // 2
    here = lax.axis_index("mp")
    place = jnp.stack([here // 2, here % 2]).astype(jnp.int32)
    chunk = jax.ShapeDtypeStruct((n_chips, tokens, head_dim), jnp.float32)
    chunk_spec = pl.BlockSpec((1, tokens, head_dim), lambda k, place: (k, 0, 0))
    keep, send = pl.pallas_call(
        project_kernel,
        grid_spec=pltpu.PrefetchScalarGridSpec(
            num_scalar_prefetch=1,
            grid=(n_chips,),
            in_specs=[
                pl.BlockSpec((tokens, width_dev), lambda k, place: (0, 0)),
                pl.BlockSpec(
                    (width_dev, 2 * head_dim), lambda k, place: (0, lax.rem(place[0] + k, n_chips))
                ),
            ],
            out_specs=[chunk_spec, chunk_spec],
        ),
        out_shape=[chunk, chunk],
        compiler_params=small_vmem,
        cost_estimate=pl.CostEstimate(
            flops=2 * tokens * width_dev * value_weight_matrix.shape[1],
            bytes_accessed=10 * 1024 * 1024,
            transcendentals=0,
        ),
    )(place, flat_hidden, value_weight_matrix)
    core_pairs = [(i, i ^ 1) for i in range(n_mp)]
    along_y = lambda k: [(i, (i + 2 * k) % n_mp) for i in range(n_mp)]
    paired = keep + lax.ppermute(send, "mp", core_pairs)
    mine, row_cache_length, paired = lax.optimization_barrier((mine, row_cache_length, paired))
    steps_ab = lax.all_to_all(mine, "dp", 0, 0, tiled=True)
    base_parts = [paired[0]] + [
        lax.ppermute(paired[k], "mp", along_y(k)) for k in range(1, n_chips)
    ]

    blocks = 4
    block_rows = rows_dev // blocks
    n_queries = step_count * group_size
    by_row = jax.ShapeDtypeStruct((rows_dev * n_queries, head_dim), jnp.float32)
    by_row_spec = pl.BlockSpec((block_rows * n_queries, head_dim), lambda i, _: (i, 0))
    cache_spec = pl.BlockSpec((block_rows, ctx_len, head_dim), lambda i, _: (i, 0, 0))
    keys_new = rotated_token_keys.astype(jnp.float32).transpose(1, 0, 2)
    cache_part, fresh_weights = pl.pallas_call(
        cache_kernel,
        grid_spec=pltpu.PrefetchScalarGridSpec(
            num_scalar_prefetch=1,
            grid=(blocks,),
            in_specs=[
                pl.BlockSpec(
                    (step_count, block_rows, group_size * head_dim), lambda i, _: (0, i, 0)
                ),
                pl.BlockSpec((block_rows * step_count, head_dim), lambda i, _: (i, 0)),
                cache_spec,
                cache_spec,
            ],
            out_specs=[
                by_row_spec,
                pl.BlockSpec((block_rows * n_queries, head_dim), lambda i, _: (0, 0)),
            ],
            scratch_shapes=[pltpu.VMEM((block_rows * n_queries, head_dim), jnp.float32)],
        ),
        out_shape=[
            by_row,
            jax.ShapeDtypeStruct((block_rows * n_queries, head_dim), jnp.float32),
        ],
        compiler_params=small_vmem,
        cost_estimate=pl.CostEstimate(
            flops=2 * 2 * 2 * rows_dev * n_queries * ctx_len * head_dim,
            bytes_accessed=10 * 1024 * 1024,
            transcendentals=rows_dev * n_queries * ctx_len,
        ),
    )(
        row_cache_length,
        queries,
        keys_new.reshape(rows_dev * step_count, head_dim),
        stored_key_cache[:, 0],
        stored_value_cache[:, 0],
    )

    base = (base_parts[0] + base_parts[1]) + (base_parts[2] + base_parts[3])
    steps_ab, cache_part, fresh_weights, base = lax.optimization_barrier(
        (steps_ab, cache_part, fresh_weights, base)
    )
    inner, new_b = pl.pallas_call(
        inner_kernel,
        out_shape=[
            jax.ShapeDtypeStruct((rank, tokens), jnp.float32),
            jax.ShapeDtypeStruct((rank, head_dim), jnp.float32),
        ],
        in_specs=[pl.BlockSpec(memory_space=pltpu.VMEM)] * 3
        + [pl.BlockSpec(memory_space=pltpu.HBM)],
        out_specs=[pl.BlockSpec(memory_space=pltpu.VMEM)] * 2,
        scratch_shapes=[
            pltpu.VMEM((8, tokens, width_dev // 8), jnp.bfloat16),
            pltpu.SemaphoreType.DMA((8,)),
        ],
        compiler_params=small_vmem,
        cost_estimate=pl.CostEstimate(
            flops=4 * tokens * width_dev * rank, bytes_accessed=1024 * 1024, transcendentals=0
        ),
    )(adapter_down_factor, adapter_up_factor.T, steps_ab, flat_hidden)
    inner = inner + lax.ppermute(inner, "mp", core_pairs)
    inner_parts = [inner] + [lax.ppermute(inner, "mp", along_y(k)) for k in range(1, n_chips)]

    by_query = (blocks, n_queries, block_rows, head_dim)

    whole = lambda a: pl.BlockSpec(a.shape, lambda t: (0,) * a.ndim)
    small = [base, *inner_parts, new_b]
    part_spec = pl.BlockSpec((blocks, group_size, block_rows, head_dim), lambda t: (0, t, 0, 0))
    weight_spec = pl.BlockSpec((group_size, block_rows, head_dim), lambda t: (t, 0, 0))
    return pl.pallas_call(
        finish_kernel,
        grid=(step_count,),
        out_shape=jax.ShapeDtypeStruct(queries.shape, jnp.bfloat16),
        in_specs=[whole(a) for a in small] + [weight_spec, part_spec],
        out_specs=pl.BlockSpec((1, rows_dev, group_size * head_dim), lambda t: (t, 0, 0)),
        scratch_shapes=[pltpu.VMEM((step_count, rows_dev, head_dim), jnp.float32)],
        compiler_params=small_vmem,
    )(*small, fresh_weights.reshape(by_query[1:]), cache_part.reshape(by_query))


def solution(mesh):
    placed = (
        P(None, "dp", "mp"),
        P(None, "dp", "mp"),
        P(None, "dp", "mp"),
        P("dp", "mp", None, None),
        P("dp", "mp", None, None),
        P("dp"),
        P("mp", None),
        P(None, "mp"),
        P("dp", None, "mp"),
        P("mp", None),
        P("dp", "mp", None),
    )
    return jax.shard_map(
        shards, mesh=mesh, in_specs=placed, out_specs=P(None, "dp", "mp"), check_vma=False
    )
```

```python
import functools

import jax
import jax.numpy as jnp
from jax import lax
from jax.experimental import pallas as pl
from jax.experimental.pallas import tpu as pltpu
from jax.sharding import PartitionSpec as P

LEARNING_RATE = 0.5
ADAPTER_SCALE = 0.5


def split_bf16(x):
    high = x.astype(jnp.bfloat16)
    low = (x - high.astype(jnp.float32)).astype(jnp.bfloat16)
    return high, low


def project_kernel(place_ref, hidden_ref, weight_ref, keep_ref, send_ref):
    dim = keep_ref.shape[2]
    both = jnp.dot(hidden_ref[...], weight_ref[...], preferred_element_type=jnp.float32)
    first, second = both[:, :dim], both[:, dim:]
    odd = place_ref[1] == 1
    keep_ref[0] = jnp.where(odd, second, first)
    send_ref[0] = jnp.where(odd, first, second)


def terms_kernel(a_ref, b_ref, out_ref):
    width = a_ref.shape[1]
    slices, depth = out_ref.shape[:2]
    a = -LEARNING_RATE * a_ref[...].astype(jnp.float32)
    b = -LEARNING_RATE * b_ref[...].astype(jnp.float32)
    for i in range(slices):
        at = slice(i * depth, (i + 1) * depth)
        out_ref[i, :, :width] = a[at]
        out_ref[i, :, width:] = b[at]


def sum_kernel(in_ref, out_ref):
    total = jnp.sum(in_ref[...], axis=0, keepdims=True)
    out_ref[...] = jnp.broadcast_to(total, out_ref.shape)


def inner_kernel(a_ref, b_ref, step_ref, hidden_ref, inner_ref, new_b_ref):
    rank, width = a_ref.shape
    steps = jnp.concatenate([step_ref[i] for i in range(step_ref.shape[0])], axis=0)
    new_b_ref[...] = b_ref[...] + steps[:, width:]
    new_a = a_ref[...] + steps[:, :width]
    parts = jnp.concatenate(split_bf16(new_a), axis=0)
    both = lax.dot_general(
        hidden_ref[...], parts, (((1,), (1,)), ((), ())), preferred_element_type=jnp.float32
    )
    both = both.T
    inner_ref[...] = both[:rank] + both[rank:]


def add_kernel(keep_ref, received_ref, *out_refs):
    for k, out_ref in enumerate(out_refs):
        out_ref[...] = keep_ref[k] + received_ref[k]


def cache_kernel(length_ref, query_ref, fresh_ref, key_ref, value_ref, part_ref, weight_ref, rows_ref, *scratch):
    pair_ref, old_ref, new_ref, old_weight_ref, new_weight_ref = scratch
    block = pl.program_id(0)
    steps, rows, width = query_ref.shape
    first = block * rows
    ctx, dim = key_ref.shape[1:]
    heads = width // dim
    n_queries = steps * heads
    scale = 1.0 / (dim**0.5)
    for t in range(steps):
        for g in range(heads):
            at = (t * heads + g) * rows
            rows_ref[at : at + rows] = query_ref[t, :, g * dim : (g + 1) * dim].astype(jnp.float32)

    @pl.when(block == 0)
    def _():
        weight_ref[...] = jnp.zeros_like(weight_ref)

    pairs = rows // 2
    lanes = 2 * ctx
    for r in range(rows):
        row = rows_ref[pl.ds(r, n_queries, stride=rows), :]
        pair_ref[r * n_queries : (r + 1) * n_queries] = row.astype(jnp.bfloat16)
    by_lane = (((1,), (1,)), ((), ()))
    mm = functools.partial(
        lax.dot_general, dimension_numbers=by_lane, preferred_element_type=jnp.float32
    )
    fresh_keys = fresh_ref[...].astype(jnp.bfloat16)
    both = 2 * n_queries
    for p in range(pairs):
        at = slice(p * both, (p + 1) * both)
        keys = key_ref[2 * p : 2 * p + 2].reshape(lanes, dim)
        old_ref[at] = mm(pair_ref[at], keys)
        new_ref[at] = mm(pair_ref[at], fresh_keys)

    lane = lax.broadcasted_iota(jnp.int32, (n_queries, lanes), 1)
    step_of = lax.broadcasted_iota(jnp.int32, (n_queries, lanes), 0) >> 3
    for r in range(rows):
        half = r % 2
        at = slice(r * n_queries, (r + 1) * n_queries)
        live = (lane >= half * ctx) & (lane < half * ctx + length_ref[first + r])
        causal = (lane >= steps * r) & (lane <= steps * r + step_of)
        old = jnp.where(live, old_ref[at] * scale, -jnp.inf)
        new = jnp.where(causal, new_ref[at] * scale, -jnp.inf)
        top = jnp.max(jnp.maximum(old, new), axis=1, keepdims=True)
        old, new = jnp.exp(old - top), jnp.exp(new - top)
        inverse = 1.0 / jnp.sum(old + new, axis=1, keepdims=True)
        old_weight_ref[at] = (old * inverse).astype(jnp.bfloat16)
        new_weight_ref[at] = (new * inverse).astype(jnp.bfloat16)

    source = lax.broadcasted_iota(jnp.int32, (lanes, lanes), 0)
    target = lax.broadcasted_iota(jnp.int32, (lanes, lanes), 1)
    move = (target - steps * block == source % steps).astype(jnp.bfloat16)
    for p in range(pairs):
        at = slice(p * both, (p + 1) * both)
        values = value_ref[2 * p : 2 * p + 2].reshape(lanes, dim)
        old_ref[at] = jnp.dot(old_weight_ref[at], values, preferred_element_type=jnp.float32)
        new_ref[at] = jnp.dot(new_weight_ref[at], move, preferred_element_type=jnp.float32)
    for q in range(n_queries):
        at = slice(q * rows, (q + 1) * rows)
        query = pl.ds(q, rows, stride=n_queries)
        part_ref[at] = old_ref[query, :]
        weight_ref[at] = weight_ref[at] + new_ref[query, :]


def finish_kernel(base_ref, u0, u1, u2, u3, b_ref, w_ref, cache_ref, out_ref, value_ref):
    t = pl.program_id(0)
    steps, rows, dim = value_ref.shape
    blocks, queries, block_rows = cache_ref.shape[:3]
    heads = queries // steps

    @pl.when(t == 0)
    def _():
        u = (u0[...] + u1[...]) + (u2[...] + u3[...])
        u_high, u_low = split_bf16(u)
        b_high, b_low = split_bf16(b_ref[...])
        dims = (((0,), (0,)), ((), ()))
        mm = functools.partial(
            lax.dot_general, dimension_numbers=dims, preferred_element_type=jnp.float32
        )
        delta = mm(u_high, b_high) + (mm(u_low, b_high) + mm(u_high, b_low))
        values = base_ref[...] + ADAPTER_SCALE * delta
        values = values.astype(jnp.bfloat16).astype(jnp.float32)
        for s in range(steps):
            value_ref[s] = values[s * rows : (s + 1) * rows]

    for step in range(steps):

        @pl.when(t == step)
        def _():
            for g in range(heads):
                for i in range(blocks):
                    at = slice(i * block_rows, (i + 1) * block_rows)
                    acc = cache_ref[i, step * heads + g]
                    weight = w_ref[step * heads + g]
                    for s in range(step + 1):
                        lane = i * steps + s
                        acc = acc + weight[:, lane : lane + 1] * value_ref[s, at]
                    out_ref[0, at, g * dim : (g + 1) * dim] = acc.astype(out_ref.dtype)


def shards(
    hidden,
    queries,
    rotated_token_keys,
    stored_key_cache,
    stored_value_cache,
    row_cache_length,
    value_weight_matrix,
    adapter_down_factor,
    learner_down_gradient,
    adapter_up_factor,
    learner_up_gradient,
):
    step_count, rows_dev, width_dev = hidden.shape
    heads_dev, ctx_len, head_dim = stored_key_cache.shape[1:]
    group_size = queries.shape[2] // (heads_dev * head_dim)
    rank = adapter_down_factor.shape[0]
    n_dp = lax.axis_size("dp")
    n_mp = lax.axis_size("mp")
    tokens = step_count * rows_dev
    flat_hidden = hidden.reshape(tokens, width_dev)

    small_vmem = pltpu.CompilerParams(vmem_limit_bytes=16 * 1024 * 1024)

    slices = jax.ShapeDtypeStruct((n_dp, rank // n_dp, width_dev + head_dim), jnp.float32)
    terms = pl.pallas_call(terms_kernel, out_shape=slices, compiler_params=small_vmem)(
        learner_down_gradient[0], learner_up_gradient[0].T
    )
    mine = lax.all_to_all(terms, "dp", 0, 0, tiled=True)
    mine = pl.pallas_call(sum_kernel, out_shape=slices, compiler_params=small_vmem)(mine)

    n_chips = n_mp // 2
    here = lax.axis_index("mp")
    place = jnp.stack([here // 2, here % 2]).astype(jnp.int32)
    chunk = jax.ShapeDtypeStruct((n_chips, tokens, head_dim), jnp.float32)
    chunk_spec = pl.BlockSpec((1, tokens, head_dim), lambda k, place: (k, 0, 0))
    keep, send = pl.pallas_call(
        project_kernel,
        grid_spec=pltpu.PrefetchScalarGridSpec(
            num_scalar_prefetch=1,
            grid=(n_chips,),
            in_specs=[
                pl.BlockSpec((tokens, width_dev), lambda k, place: (0, 0)),
                pl.BlockSpec(
                    (width_dev, 2 * head_dim), lambda k, place: (0, lax.rem(place[0] + k, n_chips))
                ),
            ],
            out_specs=[chunk_spec, chunk_spec],
        ),
        out_shape=[chunk, chunk],
        compiler_params=small_vmem,
        cost_estimate=pl.CostEstimate(
            flops=2 * tokens * width_dev * value_weight_matrix.shape[1],
            bytes_accessed=10 * 1024 * 1024,
            transcendentals=0,
        ),
    )(place, flat_hidden, value_weight_matrix)
    core_pairs = [(i, i ^ 1) for i in range(n_mp)]
    along_y = lambda k: [(i, (i + 2 * k) % n_mp) for i in range(n_mp)]
    paired = pl.pallas_call(
        add_kernel,
        out_shape=[jax.ShapeDtypeStruct((tokens, head_dim), jnp.float32)] * n_chips,
        compiler_params=small_vmem,
    )(keep, lax.ppermute(send, "mp", core_pairs))
    mine, row_cache_length, paired = lax.optimization_barrier((mine, row_cache_length, paired))
    steps_ab = lax.all_to_all(mine, "dp", 0, 0, tiled=True)
    base_parts = [paired[0]] + [
        lax.ppermute(paired[k], "mp", along_y(k)) for k in range(1, n_chips)
    ]

    blocks = 4
    f32, bf16 = jnp.float32, jnp.bfloat16
    block_rows = rows_dev // blocks
    n_queries = step_count * group_size
    by_row = jax.ShapeDtypeStruct((rows_dev * n_queries, head_dim), jnp.float32)
    by_row_spec = pl.BlockSpec((block_rows * n_queries, head_dim), lambda i, _: (i, 0))
    cache_spec = pl.BlockSpec((block_rows, ctx_len, head_dim), lambda i, _: (i, 0, 0))
    keys_new = rotated_token_keys.astype(jnp.float32).transpose(1, 0, 2)
    cache_part, fresh_weights = pl.pallas_call(
        cache_kernel,
        grid_spec=pltpu.PrefetchScalarGridSpec(
            num_scalar_prefetch=1,
            grid=(blocks,),
            in_specs=[
                pl.BlockSpec(
                    (step_count, block_rows, group_size * head_dim), lambda i, _: (0, i, 0)
                ),
                pl.BlockSpec((block_rows * step_count, head_dim), lambda i, _: (i, 0)),
                cache_spec,
                cache_spec,
            ],
            out_specs=[
                by_row_spec,
                pl.BlockSpec((block_rows * n_queries, head_dim), lambda i, _: (0, 0)),
            ],
            scratch_shapes=[
                pltpu.VMEM((block_rows * n_queries, head_dim), kind)
                for kind in (f32, bf16, f32, f32, bf16, bf16)
            ],
        ),
        out_shape=[
            by_row,
            jax.ShapeDtypeStruct((block_rows * n_queries, head_dim), jnp.float32),
        ],
        compiler_params=pltpu.CompilerParams(vmem_limit_bytes=60 * 1024 * 1024),
        cost_estimate=pl.CostEstimate(
            flops=2 * 2 * 2 * rows_dev * n_queries * ctx_len * head_dim,
            bytes_accessed=10 * 1024 * 1024,
            transcendentals=rows_dev * n_queries * ctx_len,
        ),
    )(
        row_cache_length,
        queries,
        keys_new.reshape(rows_dev * step_count, head_dim),
        stored_key_cache[:, 0],
        stored_value_cache[:, 0],
    )

    base = (base_parts[0] + base_parts[1]) + (base_parts[2] + base_parts[3])
    steps_ab, cache_part, fresh_weights, base = lax.optimization_barrier(
        (steps_ab, cache_part, fresh_weights, base)
    )
    inner, new_b = pl.pallas_call(
        inner_kernel,
        out_shape=[
            jax.ShapeDtypeStruct((rank, tokens), jnp.float32),
            jax.ShapeDtypeStruct((rank, head_dim), jnp.float32),
        ],
        compiler_params=small_vmem,
        cost_estimate=pl.CostEstimate(
            flops=4 * tokens * width_dev * rank, bytes_accessed=1024 * 1024, transcendentals=0
        ),
    )(adapter_down_factor, adapter_up_factor.T, steps_ab, flat_hidden)
    inner = inner + lax.ppermute(inner, "mp", core_pairs)
    inner_parts = [inner] + [lax.ppermute(inner, "mp", along_y(k)) for k in range(1, n_chips)]

    by_query = (blocks, n_queries, block_rows, head_dim)

    operands = [base, *inner_parts, new_b, fresh_weights.reshape(by_query[1:]), cache_part.reshape(by_query)]
    return pl.pallas_call(
        finish_kernel,
        grid=(step_count,),
        out_shape=jax.ShapeDtypeStruct(queries.shape, jnp.bfloat16),
        in_specs=[pl.BlockSpec(memory_space=pltpu.VMEM)] * len(operands),
        out_specs=pl.BlockSpec((1, rows_dev, group_size * head_dim), lambda t: (t, 0, 0)),
        scratch_shapes=[pltpu.VMEM((step_count, rows_dev, head_dim), jnp.float32)],
        compiler_params=small_vmem,
    )(*operands)


def solution(mesh):
    placed = (
        P(None, "dp", "mp"),
        P(None, "dp", "mp"),
        P(None, "dp", "mp"),
        P("dp", "mp", None, None),
        P("dp", "mp", None, None),
        P("dp"),
        P("mp", None),
        P(None, "mp"),
        P("dp", None, "mp"),
        P("mp", None),
        P("dp", "mp", None),
    )
    return jax.shard_map(
        shards, mesh=mesh, in_specs=placed, out_specs=P(None, "dp", "mp"), check_vma=False
    )
```

```python
import functools

import jax
import jax.numpy as jnp
from jax import lax
from jax.experimental import pallas as pl
from jax.experimental.pallas import tpu as pltpu
from jax.sharding import PartitionSpec as P

LEARNING_RATE = 0.5
ADAPTER_SCALE = 0.5


def split_bf16(x):
    high = x.astype(jnp.bfloat16)
    low = (x - high.astype(jnp.float32)).astype(jnp.bfloat16)
    return high, low


def project_kernel(place_ref, hidden_ref, weight_ref, keep_ref, send_ref):
    dim = keep_ref.shape[2]
    both = jnp.dot(hidden_ref[...], weight_ref[...], preferred_element_type=jnp.float32)
    first, second = both[:, :dim], both[:, dim:]
    odd = place_ref[1] == 1
    keep_ref[0] = jnp.where(odd, second, first)
    send_ref[0] = jnp.where(odd, first, second)


def terms_kernel(a_ref, b_ref, out_ref):
    width = a_ref.shape[1]
    slices, depth = out_ref.shape[:2]
    a = -LEARNING_RATE * a_ref[...].astype(jnp.float32)
    b = -LEARNING_RATE * b_ref[...].astype(jnp.float32)
    for i in range(slices):
        at = slice(i * depth, (i + 1) * depth)
        out_ref[i, :, :width] = a[at]
        out_ref[i, :, width:] = b[at]


def sum_kernel(in_ref, out_ref):
    total = jnp.sum(in_ref[...], axis=0, keepdims=True)
    out_ref[...] = jnp.broadcast_to(total, out_ref.shape)


def inner_kernel(a_ref, b_ref, step_ref, hidden_ref, inner_ref, new_b_ref):
    rank, width = a_ref.shape
    steps = jnp.concatenate([step_ref[i] for i in range(step_ref.shape[0])], axis=0)
    new_b_ref[...] = b_ref[...] + steps[:, width:]
    new_a = a_ref[...] + steps[:, :width]
    parts = jnp.concatenate(split_bf16(new_a), axis=0)
    both = lax.dot_general(
        hidden_ref[...], parts, (((1,), (1,)), ((), ())), preferred_element_type=jnp.float32
    )
    both = both.T
    inner_ref[...] = both[:rank] + both[rank:]


def add_kernel(keep_ref, received_ref, *out_refs):
    for k, out_ref in enumerate(out_refs):
        out_ref[...] = keep_ref[k] + received_ref[k]


def cache_kernel(
    offset, length_ref, query_ref, fresh_ref, key_ref, value_ref, part_ref, weight_ref, *scratch
):
    rows_ref, pair_ref, old_ref, new_ref, old_weight_ref = scratch
    steps, rows, width = query_ref.shape
    first = (pl.program_id(0) + offset) * rows
    ctx, dim = key_ref.shape[1:]
    heads = width // dim
    n_queries = steps * heads
    scale = 1.0 / (dim**0.5)
    for t in range(steps):
        for g in range(heads):
            at = (t * heads + g) * rows
            rows_ref[at : at + rows] = query_ref[t, :, g * dim : (g + 1) * dim].astype(jnp.float32)
    pairs = rows // 2
    lanes = 2 * ctx
    for r in range(rows):
        row = rows_ref[pl.ds(r, n_queries, stride=rows), :]
        pair_ref[r * n_queries : (r + 1) * n_queries] = row.astype(jnp.bfloat16)
    by_lane = (((1,), (1,)), ((), ()))
    mm = functools.partial(
        lax.dot_general, dimension_numbers=by_lane, preferred_element_type=jnp.float32
    )
    fresh_keys = fresh_ref[...].reshape(steps * rows, dim)
    both = 2 * n_queries
    for p in range(pairs):
        at = slice(p * both, (p + 1) * both)
        keys = key_ref[2 * p : 2 * p + 2].reshape(lanes, dim)
        old_ref[at] = mm(pair_ref[at], keys)
        new_ref[at] = mm(pair_ref[at], fresh_keys)

    lane = lax.broadcasted_iota(jnp.int32, (n_queries, lanes), 1)
    step_of = lax.broadcasted_iota(jnp.int32, (n_queries, lanes), 0) // heads
    row_of, reached = lane % rows, lane // rows <= step_of
    for r in range(rows):
        half = r % 2
        at = slice(r * n_queries, (r + 1) * n_queries)
        live = (lane >= half * ctx) & (lane < half * ctx + length_ref[first + r])
        causal = (row_of == r) & reached
        old = jnp.where(live, old_ref[at] * scale, -jnp.inf)
        new = jnp.where(causal, new_ref[at] * scale, -jnp.inf)
        top = jnp.max(jnp.maximum(old, new), axis=1, keepdims=True)
        old, new = jnp.exp(old - top), jnp.exp(new - top)
        inverse = 1.0 / jnp.sum(old + new, axis=1, keepdims=True)
        old_weight_ref[at] = (old * inverse).astype(jnp.bfloat16)
        new_ref[at] = new * inverse

    for p in range(pairs):
        at = slice(p * both, (p + 1) * both)
        values = value_ref[2 * p : 2 * p + 2].reshape(lanes, dim)
        old_ref[at] = jnp.dot(old_weight_ref[at], values, preferred_element_type=jnp.float32)
    for q in range(n_queries):
        at = slice(q * rows, (q + 1) * rows)
        query = pl.ds(q, rows, stride=n_queries)
        part_ref[at] = old_ref[query, :]
        weight_ref[at] = new_ref[query, :].astype(jnp.bfloat16)


def finish_kernel(v0, v1, v2, v3, u0, u1, u2, u3, b_ref, *refs):
    *halves, out_ref, value_ref = refs
    t = pl.program_id(0)
    blocks, lanes, dim = value_ref.shape
    steps = pl.num_programs(0)
    rows = out_ref.shape[1]
    block_rows = rows // blocks
    heads = out_ref.shape[2] // dim

    @pl.when(t == 0)
    def _():
        u = (u0[...] + u1[...]) + (u2[...] + u3[...])
        u_high, u_low = split_bf16(u)
        b_high, b_low = split_bf16(b_ref[...])
        dims = (((0,), (0,)), ((), ()))
        mm = functools.partial(
            lax.dot_general, dimension_numbers=dims, preferred_element_type=jnp.float32
        )
        delta = mm(u_high, b_high) + (mm(u_low, b_high) + mm(u_high, b_low))
        values = (v0[...] + v1[...]) + (v2[...] + v3[...]) + ADAPTER_SCALE * delta
        values = values.astype(jnp.bfloat16)
        for i in range(blocks):
            for s in range(lanes // block_rows):
                at = s * rows + i * block_rows
                value_ref[i, s * block_rows : (s + 1) * block_rows] = values[at : at + block_rows]

    size = heads * block_rows
    start = pl.multiple_of(t * size, size)
    half = blocks // 2
    for i in range(blocks):
        part_ref, weight_ref = halves[2 * (i // half) : 2 * (i // half) + 2]
        fresh = jnp.dot(
            weight_ref[i % half, pl.ds(start, size), :], value_ref[i], preferred_element_type=jnp.float32
        )
        context = part_ref[i % half, pl.ds(start, size), :] + fresh
        for g in range(heads):
            out_ref[0, i * block_rows : (i + 1) * block_rows, g * dim : (g + 1) * dim] = context[
                g * block_rows : (g + 1) * block_rows
            ].astype(out_ref.dtype)


def shards(
    hidden,
    queries,
    rotated_token_keys,
    stored_key_cache,
    stored_value_cache,
    row_cache_length,
    value_weight_matrix,
    adapter_down_factor,
    learner_down_gradient,
    adapter_up_factor,
    learner_up_gradient,
):
    step_count, rows_dev, width_dev = hidden.shape
    heads_dev, ctx_len, head_dim = stored_key_cache.shape[1:]
    group_size = queries.shape[2] // (heads_dev * head_dim)
    rank = adapter_down_factor.shape[0]
    n_dp = lax.axis_size("dp")
    n_mp = lax.axis_size("mp")
    tokens = step_count * rows_dev
    flat_hidden = hidden.reshape(tokens, width_dev)

    small_vmem = pltpu.CompilerParams(vmem_limit_bytes=16 * 1024 * 1024)

    slices = jax.ShapeDtypeStruct((n_dp, rank // n_dp, width_dev + head_dim), jnp.float32)
    terms = pl.pallas_call(
        terms_kernel,
        out_shape=slices,
        compiler_params=pltpu.CompilerParams(vmem_limit_bytes=60 * 1024 * 1024),
    )(
        learner_down_gradient[0], learner_up_gradient[0].T
    )
    mine = lax.all_to_all(terms, "dp", 0, 0, tiled=True)
    mine = pl.pallas_call(sum_kernel, out_shape=slices, compiler_params=small_vmem)(mine)

    n_chips = n_mp // 2
    here = lax.axis_index("mp")
    place = jnp.stack([here // 2, here % 2]).astype(jnp.int32)
    chunk = jax.ShapeDtypeStruct((n_chips, tokens, head_dim), jnp.float32)
    chunk_spec = pl.BlockSpec((1, tokens, head_dim), lambda k, place: (k, 0, 0))
    keep, send = pl.pallas_call(
        project_kernel,
        grid_spec=pltpu.PrefetchScalarGridSpec(
            num_scalar_prefetch=1,
            grid=(n_chips,),
            in_specs=[
                pl.BlockSpec((tokens, width_dev), lambda k, place: (0, 0)),
                pl.BlockSpec(
                    (width_dev, 2 * head_dim), lambda k, place: (0, lax.rem(place[0] + k, n_chips))
                ),
            ],
            out_specs=[chunk_spec, chunk_spec],
        ),
        out_shape=[chunk, chunk],
        compiler_params=small_vmem,
        cost_estimate=pl.CostEstimate(
            flops=2 * tokens * width_dev * value_weight_matrix.shape[1],
            bytes_accessed=10 * 1024 * 1024,
            transcendentals=0,
        ),
    )(place, flat_hidden, value_weight_matrix)
    core_pairs = [(i, i ^ 1) for i in range(n_mp)]
    along_y = lambda k: [(i, (i + 2 * k) % n_mp) for i in range(n_mp)]
    paired = pl.pallas_call(
        add_kernel,
        out_shape=[jax.ShapeDtypeStruct((tokens, head_dim), jnp.float32)] * n_chips,
        compiler_params=small_vmem,
    )(keep, lax.ppermute(send, "mp", core_pairs))
    mine, row_cache_length, paired = lax.optimization_barrier((mine, row_cache_length, paired))
    steps_ab = lax.all_to_all(mine, "dp", 0, 0, tiled=True)
    base_parts = [paired[0]] + [
        lax.ppermute(paired[k], "mp", along_y(k)) for k in range(1, n_chips)
    ]

    blocks = 4
    half = blocks // 2
    block_rows = rows_dev // blocks
    n_queries = step_count * group_size
    size = block_rows * n_queries

    def attend(offset, lengths, vmem_mib):
        by_row = lambda kind: jax.ShapeDtypeStruct((half * size, head_dim), kind)
        by_row_spec = pl.BlockSpec((size, head_dim), lambda i, _: (i, 0))
        cache_spec = pl.BlockSpec((block_rows, ctx_len, head_dim), lambda i, _: (i + offset, 0, 0))
        token_spec = lambda width: pl.BlockSpec(
            (step_count, block_rows, width), lambda i, _: (0, i + offset, 0)
        )
        f32, bf16 = jnp.float32, jnp.bfloat16
        part, weights = pl.pallas_call(
            functools.partial(cache_kernel, offset),
            grid_spec=pltpu.PrefetchScalarGridSpec(
                num_scalar_prefetch=1,
                grid=(half,),
                in_specs=[
                    token_spec(group_size * head_dim),
                    token_spec(head_dim),
                    cache_spec,
                    cache_spec,
                ],
                out_specs=[by_row_spec, by_row_spec],
                scratch_shapes=[
                    pltpu.VMEM((size, head_dim), kind) for kind in (f32, bf16, f32, f32, bf16)
                ],
            ),
            out_shape=[by_row(f32), by_row(bf16)],
            compiler_params=pltpu.CompilerParams(vmem_limit_bytes=vmem_mib * 1024 * 1024),
            cost_estimate=pl.CostEstimate(
                flops=2 * 2 * half * size * 2 * ctx_len * head_dim,
                bytes_accessed=5 * 1024 * 1024,
                transcendentals=2 * half * size * head_dim,
            ),
        )(lengths, queries, rotated_token_keys, stored_key_cache[:, 0], stored_value_cache[:, 0])
        return part.reshape(half, size, head_dim), weights.reshape(half, size, head_dim)

    first_half = attend(0, row_cache_length, 60)
    steps_ab, first_half, base_parts = lax.optimization_barrier((steps_ab, first_half, base_parts))

    inner, new_b = pl.pallas_call(
        inner_kernel,
        out_shape=[
            jax.ShapeDtypeStruct((rank, tokens), jnp.float32),
            jax.ShapeDtypeStruct((rank, head_dim), jnp.float32),
        ],
        compiler_params=small_vmem,
        cost_estimate=pl.CostEstimate(
            flops=4 * tokens * width_dev * rank, bytes_accessed=1024 * 1024, transcendentals=0
        ),
    )(adapter_down_factor, adapter_up_factor.T, steps_ab, flat_hidden)
    inner = inner + lax.ppermute(inner, "mp", core_pairs)
    inner, row_cache_length = lax.optimization_barrier((inner, row_cache_length))
    second_half = attend(half, row_cache_length, 52)
    inner_parts = [inner] + [lax.ppermute(inner, "mp", along_y(k)) for k in range(1, n_chips)]

    operands = [*base_parts, *inner_parts, new_b, *first_half, *second_half]
    return pl.pallas_call(
        finish_kernel,
        grid=(step_count,),
        out_shape=jax.ShapeDtypeStruct(queries.shape, jnp.bfloat16),
        in_specs=[pl.BlockSpec(memory_space=pltpu.VMEM)] * len(operands),
        out_specs=pl.BlockSpec((1, rows_dev, group_size * head_dim), lambda t: (t, 0, 0)),
        scratch_shapes=[pltpu.VMEM((blocks, step_count * block_rows, head_dim), jnp.bfloat16)],
        compiler_params=small_vmem,
    )(*operands)


def solution(mesh):
    placed = (
        P(None, "dp", "mp"),
        P(None, "dp", "mp"),
        P(None, "dp", "mp"),
        P("dp", "mp", None, None),
        P("dp", "mp", None, None),
        P("dp"),
        P("mp", None),
        P(None, "mp"),
        P("dp", None, "mp"),
        P("mp", None),
        P("dp", "mp", None),
    )
    return jax.shard_map(
        shards, mesh=mesh, in_specs=placed, out_specs=P(None, "dp", "mp"), check_vma=False
    )
```

```python
import functools

import jax
import jax.numpy as jnp
from jax import lax
from jax.experimental import pallas as pl
from jax.experimental.pallas import tpu as pltpu
from jax.sharding import PartitionSpec as P

LEARNING_RATE = 0.5
ADAPTER_SCALE = 0.5


def split_bf16(x):
    high = x.astype(jnp.bfloat16)
    low = (x - high.astype(jnp.float32)).astype(jnp.bfloat16)
    return high, low


def project_kernel(place_ref, hidden_ref, weight_ref, keep_ref, send_ref):
    dim = keep_ref.shape[2]
    both = jnp.dot(hidden_ref[...], weight_ref[...], preferred_element_type=jnp.float32)
    first, second = both[:, :dim], both[:, dim:]
    odd = place_ref[1] == 1
    keep_ref[0] = jnp.where(odd, second, first)
    send_ref[0] = jnp.where(odd, first, second)


def terms_kernel(a_ref, b_ref, out_ref):
    width = a_ref.shape[1]
    slices, depth = out_ref.shape[:2]
    a = -LEARNING_RATE * a_ref[...].astype(jnp.float32)
    b = -LEARNING_RATE * b_ref[...].astype(jnp.float32)
    for i in range(slices):
        at = slice(i * depth, (i + 1) * depth)
        out_ref[i, :, :width] = a[at]
        out_ref[i, :, width:] = b[at]


def sum_kernel(in_ref, out_ref):
    total = jnp.sum(in_ref[...], axis=0, keepdims=True)
    out_ref[...] = jnp.broadcast_to(total, out_ref.shape)


def inner_kernel(a_ref, b_ref, step_ref, hidden_ref, inner_ref, new_b_ref):
    rank, width = a_ref.shape
    steps = jnp.concatenate([step_ref[i] for i in range(step_ref.shape[0])], axis=0)
    new_b_ref[...] = b_ref[...] + steps[:, width:]
    new_a = a_ref[...] + steps[:, :width]
    parts = jnp.concatenate(split_bf16(new_a), axis=0)
    both = lax.dot_general(
        hidden_ref[...], parts, (((1,), (1,)), ((), ())), preferred_element_type=jnp.float32
    )
    both = both.T
    inner_ref[...] = both[:rank] + both[rank:]


def add_kernel(keep_ref, received_ref, *out_refs):
    for k, out_ref in enumerate(out_refs):
        out_ref[...] = keep_ref[k] + received_ref[k]


def cache_kernel(
    offset, length_ref, query_ref, fresh_ref, key_ref, value_ref, part_ref, weight_ref, *scratch
):
    rows_ref, pair_ref, old_ref, new_ref, old_weight_ref = scratch
    steps, rows, width = query_ref.shape
    first = (pl.program_id(0) + offset) * rows
    ctx, dim = key_ref.shape[1:]
    heads = width // dim
    n_queries = steps * heads
    scale = 1.0 / (dim**0.5)
    for t in range(steps):
        for g in range(heads):
            at = (t * heads + g) * rows
            rows_ref[at : at + rows] = query_ref[t, :, g * dim : (g + 1) * dim].astype(jnp.float32)
    pairs = rows // 2
    lanes = 2 * ctx
    for r in range(rows):
        row = rows_ref[pl.ds(r, n_queries, stride=rows), :]
        pair_ref[r * n_queries : (r + 1) * n_queries] = row.astype(jnp.bfloat16)
    by_lane = (((1,), (1,)), ((), ()))
    mm = functools.partial(
        lax.dot_general, dimension_numbers=by_lane, preferred_element_type=jnp.float32
    )
    fresh_keys = fresh_ref[...].reshape(steps * rows, dim)
    both = 2 * n_queries
    for p in range(pairs):
        at = slice(p * both, (p + 1) * both)
        keys = key_ref[2 * p : 2 * p + 2].reshape(lanes, dim)
        old_ref[at] = mm(pair_ref[at], keys)
        new_ref[at] = mm(pair_ref[at], fresh_keys)

    lane = lax.broadcasted_iota(jnp.int32, (n_queries, lanes), 1)
    step_of = lax.broadcasted_iota(jnp.int32, (n_queries, lanes), 0) // heads
    row_of, reached = lane % rows, lane // rows <= step_of
    for r in range(rows):
        half = r % 2
        at = slice(r * n_queries, (r + 1) * n_queries)
        live = (lane >= half * ctx) & (lane < half * ctx + length_ref[first + r])
        causal = (row_of == r) & reached
        old = jnp.where(live, old_ref[at] * scale, -jnp.inf)
        new = jnp.where(causal, new_ref[at] * scale, -jnp.inf)
        top = jnp.max(jnp.maximum(old, new), axis=1, keepdims=True)
        old, new = jnp.exp(old - top), jnp.exp(new - top)
        inverse = 1.0 / jnp.sum(old + new, axis=1, keepdims=True)
        old_weight_ref[at] = (old * inverse).astype(jnp.bfloat16)
        new_ref[at] = new * inverse

    for p in range(pairs):
        at = slice(p * both, (p + 1) * both)
        values = value_ref[2 * p : 2 * p + 2].reshape(lanes, dim)
        old_ref[at] = jnp.dot(old_weight_ref[at], values, preferred_element_type=jnp.float32)
    for q in range(n_queries):
        at = slice(q * rows, (q + 1) * rows)
        query = pl.ds(q, rows, stride=n_queries)
        part_ref[at] = old_ref[query, :]
        weight_ref[at] = new_ref[query, :].astype(jnp.bfloat16)


def finish_kernel(v0, v1, v2, v3, u0, u1, u2, u3, b_ref, *refs):
    *halves, out_ref, value_ref = refs
    t = pl.program_id(0)
    blocks, lanes, dim = value_ref.shape
    steps = pl.num_programs(0)
    rows = out_ref.shape[1]
    block_rows = rows // blocks
    heads = out_ref.shape[2] // dim

    @pl.when(t == 0)
    def _():
        u = (u0[...] + u1[...]) + (u2[...] + u3[...])
        u_high, u_low = split_bf16(u)
        b_high, b_low = split_bf16(b_ref[...])
        dims = (((0,), (0,)), ((), ()))
        mm = functools.partial(
            lax.dot_general, dimension_numbers=dims, preferred_element_type=jnp.float32
        )
        delta = mm(u_high, b_high) + (mm(u_low, b_high) + mm(u_high, b_low))
        values = (v0[...] + v1[...]) + (v2[...] + v3[...]) + ADAPTER_SCALE * delta
        values = values.astype(jnp.bfloat16)
        for i in range(blocks):
            for s in range(lanes // block_rows):
                at = s * rows + i * block_rows
                value_ref[i, s * block_rows : (s + 1) * block_rows] = values[at : at + block_rows]

    size = heads * block_rows
    start = pl.multiple_of(t * size, size)
    half = blocks // 2
    for i in range(blocks):
        part_ref, weight_ref = halves[2 * (i // half) : 2 * (i // half) + 2]
        fresh = jnp.dot(
            weight_ref[i % half, pl.ds(start, size), :], value_ref[i], preferred_element_type=jnp.float32
        )
        context = part_ref[i % half, pl.ds(start, size), :] + fresh
        for g in range(heads):
            out_ref[0, i * block_rows : (i + 1) * block_rows, g * dim : (g + 1) * dim] = context[
                g * block_rows : (g + 1) * block_rows
            ].astype(out_ref.dtype)


def shards(
    hidden,
    queries,
    rotated_token_keys,
    stored_key_cache,
    stored_value_cache,
    row_cache_length,
    value_weight_matrix,
    adapter_down_factor,
    learner_down_gradient,
    adapter_up_factor,
    learner_up_gradient,
):
    step_count, rows_dev, width_dev = hidden.shape
    heads_dev, ctx_len, head_dim = stored_key_cache.shape[1:]
    group_size = queries.shape[2] // (heads_dev * head_dim)
    rank = adapter_down_factor.shape[0]
    n_dp = lax.axis_size("dp")
    n_mp = lax.axis_size("mp")
    tokens = step_count * rows_dev
    flat_hidden = hidden.reshape(tokens, width_dev)

    small_vmem = pltpu.CompilerParams(vmem_limit_bytes=16 * 1024 * 1024)

    slices = jax.ShapeDtypeStruct((n_dp, rank // n_dp, width_dev + head_dim), jnp.float32)
    terms = pl.pallas_call(
        terms_kernel,
        out_shape=slices,
        compiler_params=pltpu.CompilerParams(vmem_limit_bytes=60 * 1024 * 1024),
    )(
        learner_down_gradient[0], learner_up_gradient[0].T
    )
    mine = lax.all_to_all(terms, "dp", 0, 0, tiled=True)
    mine = pl.pallas_call(sum_kernel, out_shape=slices, compiler_params=small_vmem)(mine)

    n_chips = n_mp // 2
    here = lax.axis_index("mp")
    place = jnp.stack([here // 2, here % 2]).astype(jnp.int32)
    chunk = jax.ShapeDtypeStruct((n_chips, tokens, head_dim), jnp.float32)
    chunk_spec = pl.BlockSpec((1, tokens, head_dim), lambda k, place: (k, 0, 0))
    keep, send = pl.pallas_call(
        project_kernel,
        grid_spec=pltpu.PrefetchScalarGridSpec(
            num_scalar_prefetch=1,
            grid=(n_chips,),
            in_specs=[
                pl.BlockSpec((tokens, width_dev), lambda k, place: (0, 0)),
                pl.BlockSpec(
                    (width_dev, 2 * head_dim), lambda k, place: (0, lax.rem(place[0] + k, n_chips))
                ),
            ],
            out_specs=[chunk_spec, chunk_spec],
        ),
        out_shape=[chunk, chunk],
        compiler_params=small_vmem,
        cost_estimate=pl.CostEstimate(
            flops=2 * tokens * width_dev * value_weight_matrix.shape[1],
            bytes_accessed=10 * 1024 * 1024,
            transcendentals=0,
        ),
    )(place, flat_hidden, value_weight_matrix)
    core_pairs = [(i, i ^ 1) for i in range(n_mp)]
    along_y = lambda k: [(i, (i + 2 * k) % n_mp) for i in range(n_mp)]
    paired = pl.pallas_call(
        add_kernel,
        out_shape=[jax.ShapeDtypeStruct((tokens, head_dim), jnp.float32)] * n_chips,
        compiler_params=small_vmem,
    )(keep, lax.ppermute(send, "mp", core_pairs))
    mine, row_cache_length, _ = lax.optimization_barrier((mine, row_cache_length, paired))
    steps_ab = lax.all_to_all(mine, "dp", 0, 0, tiled=True)
    base_parts = [paired[0]] + [
        lax.ppermute(paired[k], "mp", along_y(k)) for k in range(1, n_chips)
    ]

    blocks = 4
    half = blocks // 2
    block_rows = rows_dev // blocks
    n_queries = step_count * group_size
    size = block_rows * n_queries

    def attend(offset, lengths, vmem_mib):
        by_row = lambda kind: jax.ShapeDtypeStruct((half * size, head_dim), kind)
        by_row_spec = pl.BlockSpec((size, head_dim), lambda i, _: (i, 0))
        cache_spec = pl.BlockSpec((block_rows, ctx_len, head_dim), lambda i, _: (i + offset, 0, 0))
        token_spec = lambda width: pl.BlockSpec(
            (step_count, block_rows, width), lambda i, _: (0, i + offset, 0)
        )
        f32, bf16 = jnp.float32, jnp.bfloat16
        part, weights = pl.pallas_call(
            functools.partial(cache_kernel, offset),
            grid_spec=pltpu.PrefetchScalarGridSpec(
                num_scalar_prefetch=1,
                grid=(half,),
                in_specs=[
                    token_spec(group_size * head_dim),
                    token_spec(head_dim),
                    cache_spec,
                    cache_spec,
                ],
                out_specs=[by_row_spec, by_row_spec],
                scratch_shapes=[
                    pltpu.VMEM((size, head_dim), kind) for kind in (f32, bf16, f32, f32, bf16)
                ],
            ),
            out_shape=[by_row(f32), by_row(bf16)],
            compiler_params=pltpu.CompilerParams(vmem_limit_bytes=vmem_mib * 1024 * 1024),
            cost_estimate=pl.CostEstimate(
                flops=2 * 2 * half * size * 2 * ctx_len * head_dim,
                bytes_accessed=5 * 1024 * 1024,
                transcendentals=2 * half * size * head_dim,
            ),
        )(lengths, queries, rotated_token_keys, stored_key_cache[:, 0], stored_value_cache[:, 0])
        return part.reshape(half, size, head_dim), weights.reshape(half, size, head_dim)

    first_half = attend(0, row_cache_length, 60)
    steps_ab, first_half = lax.optimization_barrier((steps_ab, first_half))

    inner, new_b = pl.pallas_call(
        inner_kernel,
        out_shape=[
            jax.ShapeDtypeStruct((rank, tokens), jnp.float32),
            jax.ShapeDtypeStruct((rank, head_dim), jnp.float32),
        ],
        compiler_params=small_vmem,
        cost_estimate=pl.CostEstimate(flops=0, bytes_accessed=0, transcendentals=0),
    )(adapter_down_factor, adapter_up_factor.T, steps_ab, flat_hidden)
    inner = inner + lax.ppermute(inner, "mp", core_pairs)
    inner, base_parts = lax.optimization_barrier((inner, base_parts))
    inner, row_cache_length = lax.optimization_barrier((inner, row_cache_length))
    second_half = attend(half, row_cache_length, 52)
    inner_parts = [inner] + [lax.ppermute(inner, "mp", along_y(k)) for k in range(1, n_chips)]

    operands = [*base_parts, *inner_parts, new_b, *first_half, *second_half]
    return pl.pallas_call(
        finish_kernel,
        grid=(step_count,),
        out_shape=jax.ShapeDtypeStruct(queries.shape, jnp.bfloat16),
        in_specs=[pl.BlockSpec(memory_space=pltpu.VMEM)] * len(operands),
        out_specs=pl.BlockSpec((1, rows_dev, group_size * head_dim), lambda t: (t, 0, 0)),
        scratch_shapes=[pltpu.VMEM((blocks, step_count * block_rows, head_dim), jnp.bfloat16)],
        compiler_params=small_vmem,
    )(*operands)


def solution(mesh):
    placed = (
        P(None, "dp", "mp"),
        P(None, "dp", "mp"),
        P(None, "dp", "mp"),
        P("dp", "mp", None, None),
        P("dp", "mp", None, None),
        P("dp"),
        P("mp", None),
        P(None, "mp"),
        P("dp", None, "mp"),
        P("mp", None),
        P("dp", "mp", None),
    )
    return jax.shard_map(
        shards, mesh=mesh, in_specs=placed, out_specs=P(None, "dp", "mp"), check_vma=False
    )
```

```python
import functools

import jax
import jax.numpy as jnp
from jax import lax
from jax.experimental import pallas as pl
from jax.experimental.pallas import tpu as pltpu
from jax.sharding import PartitionSpec as P

LEARNING_RATE = 0.5
ADAPTER_SCALE = 0.5


def split_bf16(x):
    high = x.astype(jnp.bfloat16)
    low = (x - high.astype(jnp.float32)).astype(jnp.bfloat16)
    return high, low


def project_kernel(place_ref, hidden_ref, weight_ref, keep_ref, send_ref):
    dim = keep_ref.shape[2]
    both = jnp.dot(hidden_ref[...], weight_ref[...], preferred_element_type=jnp.float32)
    first, second = both[:, :dim], both[:, dim:]
    odd = place_ref[1] == 1
    keep_ref[0] = jnp.where(odd, second, first)
    send_ref[0] = jnp.where(odd, first, second)


def terms_kernel(a_ref, b_ref, out_ref):
    width = a_ref.shape[1]
    slices, depth = out_ref.shape[:2]
    a = -LEARNING_RATE * a_ref[...].astype(jnp.float32)
    b = -LEARNING_RATE * b_ref[...].astype(jnp.float32)
    for i in range(slices):
        at = slice(i * depth, (i + 1) * depth)
        out_ref[i, :, :width] = a[at]
        out_ref[i, :, width:] = b[at]


def sum_kernel(in_ref, out_ref):
    total = jnp.sum(in_ref[...], axis=0, keepdims=True)
    out_ref[...] = jnp.broadcast_to(total, out_ref.shape)


def inner_kernel(a_ref, b_ref, step_ref, hidden_ref, inner_ref, new_b_ref):
    rank, width = a_ref.shape
    steps = jnp.concatenate([step_ref[i] for i in range(step_ref.shape[0])], axis=0)
    new_b_ref[...] = b_ref[...] + steps[:, width:]
    new_a = a_ref[...] + steps[:, :width]
    parts = jnp.concatenate(split_bf16(new_a), axis=0)
    both = lax.dot_general(
        hidden_ref[...], parts, (((1,), (1,)), ((), ())), preferred_element_type=jnp.float32
    )
    both = both.T
    inner_ref[...] = both[:rank] + both[rank:]


def add_kernel(keep_ref, received_ref, *out_refs):
    for k, out_ref in enumerate(out_refs):
        out_ref[...] = keep_ref[k] + received_ref[k]


def cache_kernel(
    offset, length_ref, query_ref, fresh_ref, key_ref, value_ref, part_ref, weight_ref, *scratch
):
    rows_ref, pair_ref, old_ref, new_ref, old_weight_ref = scratch
    steps, rows, width = query_ref.shape
    first = (pl.program_id(0) + offset) * rows
    ctx, dim = key_ref.shape[1:]
    heads = width // dim
    n_queries = steps * heads
    scale = 1.0 / (dim**0.5)
    for t in range(steps):
        for g in range(heads):
            at = (t * heads + g) * rows
            rows_ref[at : at + rows] = query_ref[t, :, g * dim : (g + 1) * dim].astype(jnp.float32)
    pairs = rows // 2
    lanes = 2 * ctx
    for r in range(rows):
        row = rows_ref[pl.ds(r, n_queries, stride=rows), :]
        pair_ref[r * n_queries : (r + 1) * n_queries] = row.astype(jnp.bfloat16)
    by_lane = (((1,), (1,)), ((), ()))
    mm = functools.partial(
        lax.dot_general, dimension_numbers=by_lane, preferred_element_type=jnp.float32
    )
    fresh_keys = fresh_ref[...].reshape(steps * rows, dim)
    both = 2 * n_queries
    for p in range(pairs):
        at = slice(p * both, (p + 1) * both)
        keys = key_ref[2 * p : 2 * p + 2].reshape(lanes, dim)
        old_ref[at] = mm(pair_ref[at], keys)
        new_ref[at] = mm(pair_ref[at], fresh_keys)

    lane = lax.broadcasted_iota(jnp.int32, (n_queries, lanes), 1)
    step_of = lax.broadcasted_iota(jnp.int32, (n_queries, lanes), 0) // heads
    row_of, reached = lane % rows, lane // rows <= step_of
    for r in range(rows):
        half = r % 2
        at = slice(r * n_queries, (r + 1) * n_queries)
        live = (lane >= half * ctx) & (lane < half * ctx + length_ref[first + r])
        causal = (row_of == r) & reached
        old = jnp.where(live, old_ref[at] * scale, -jnp.inf)
        new = jnp.where(causal, new_ref[at] * scale, -jnp.inf)
        top = jnp.max(jnp.maximum(old, new), axis=1, keepdims=True)
        old, new = jnp.exp(old - top), jnp.exp(new - top)
        inverse = 1.0 / jnp.sum(old + new, axis=1, keepdims=True)
        old_weight_ref[at] = (old * inverse).astype(jnp.bfloat16)
        new_ref[at] = new * inverse

    for p in range(pairs):
        at = slice(p * both, (p + 1) * both)
        values = value_ref[2 * p : 2 * p + 2].reshape(lanes, dim)
        old_ref[at] = jnp.dot(old_weight_ref[at], values, preferred_element_type=jnp.float32)
    for q in range(n_queries):
        at = slice(q * rows, (q + 1) * rows)
        query = pl.ds(q, rows, stride=n_queries)
        part_ref[at] = old_ref[query, :]
        weight_ref[at] = new_ref[query, :].astype(jnp.bfloat16)


def finish_kernel(v0, v1, v2, v3, u0, u1, u2, u3, b_ref, *refs):
    *halves, out_ref, value_ref, held_ref, sems = refs
    blocks, lanes, dim = value_ref.shape
    steps, rows, width = held_ref.shape
    block_rows = rows // blocks
    heads = width // dim
    u = (u0[...] + u1[...]) + (u2[...] + u3[...])
    u_high, u_low = split_bf16(u)
    b_high, b_low = split_bf16(b_ref[...])
    dims = (((0,), (0,)), ((), ()))
    mm = functools.partial(
        lax.dot_general, dimension_numbers=dims, preferred_element_type=jnp.float32
    )
    delta = mm(u_high, b_high) + (mm(u_low, b_high) + mm(u_high, b_low))
    values = (v0[...] + v1[...]) + (v2[...] + v3[...]) + ADAPTER_SCALE * delta
    values = values.astype(jnp.bfloat16)
    for i in range(blocks):
        for s in range(steps):
            at = s * rows + i * block_rows
            value_ref[i, s * block_rows : (s + 1) * block_rows] = values[at : at + block_rows]

    size = heads * block_rows
    half = blocks // 2
    copies = []
    for t in range(steps):
        at = slice(t * size, (t + 1) * size)
        for i in range(blocks):
            part_ref, weight_ref = halves[2 * (i // half) : 2 * (i // half) + 2]
            fresh = jnp.dot(
                weight_ref[i % half, at], value_ref[i], preferred_element_type=jnp.float32
            )
            context = part_ref[i % half, at] + fresh
            for g in range(heads):
                held_ref[t, i * block_rows : (i + 1) * block_rows, g * dim : (g + 1) * dim] = (
                    context[g * block_rows : (g + 1) * block_rows].astype(held_ref.dtype)
                )
        copies.append(pltpu.make_async_copy(held_ref.at[t], out_ref.at[t], sems.at[t]))
        copies[-1].start()
    for copy in copies:
        copy.wait()


def shards(
    hidden,
    queries,
    rotated_token_keys,
    stored_key_cache,
    stored_value_cache,
    row_cache_length,
    value_weight_matrix,
    adapter_down_factor,
    learner_down_gradient,
    adapter_up_factor,
    learner_up_gradient,
):
    step_count, rows_dev, width_dev = hidden.shape
    heads_dev, ctx_len, head_dim = stored_key_cache.shape[1:]
    group_size = queries.shape[2] // (heads_dev * head_dim)
    rank = adapter_down_factor.shape[0]
    n_dp = lax.axis_size("dp")
    n_mp = lax.axis_size("mp")
    tokens = step_count * rows_dev
    flat_hidden = hidden.reshape(tokens, width_dev)

    small_vmem = pltpu.CompilerParams(vmem_limit_bytes=16 * 1024 * 1024)

    slices = jax.ShapeDtypeStruct((n_dp, rank // n_dp, width_dev + head_dim), jnp.float32)
    terms = pl.pallas_call(
        terms_kernel,
        out_shape=slices,
        compiler_params=pltpu.CompilerParams(vmem_limit_bytes=60 * 1024 * 1024),
    )(
        learner_down_gradient[0], learner_up_gradient[0].T
    )
    mine = lax.all_to_all(terms, "dp", 0, 0, tiled=True)
    mine = pl.pallas_call(sum_kernel, out_shape=slices, compiler_params=small_vmem)(mine)

    n_chips = n_mp // 2
    here = lax.axis_index("mp")
    place = jnp.stack([here // 2, here % 2]).astype(jnp.int32)
    chunk = jax.ShapeDtypeStruct((n_chips, tokens, head_dim), jnp.float32)
    chunk_spec = pl.BlockSpec((1, tokens, head_dim), lambda k, place: (k, 0, 0))
    keep, send = pl.pallas_call(
        project_kernel,
        grid_spec=pltpu.PrefetchScalarGridSpec(
            num_scalar_prefetch=1,
            grid=(n_chips,),
            in_specs=[
                pl.BlockSpec((tokens, width_dev), lambda k, place: (0, 0)),
                pl.BlockSpec(
                    (width_dev, 2 * head_dim), lambda k, place: (0, lax.rem(place[0] + k, n_chips))
                ),
            ],
            out_specs=[chunk_spec, chunk_spec],
        ),
        out_shape=[chunk, chunk],
        compiler_params=small_vmem,
        cost_estimate=pl.CostEstimate(
            flops=2 * tokens * width_dev * value_weight_matrix.shape[1],
            bytes_accessed=10 * 1024 * 1024,
            transcendentals=0,
        ),
    )(place, flat_hidden, value_weight_matrix)
    core_pairs = [(i, i ^ 1) for i in range(n_mp)]
    along_y = lambda k: [(i, (i + 2 * k) % n_mp) for i in range(n_mp)]
    paired = pl.pallas_call(
        add_kernel,
        out_shape=[jax.ShapeDtypeStruct((tokens, head_dim), jnp.float32)] * n_chips,
        compiler_params=small_vmem,
    )(keep, lax.ppermute(send, "mp", core_pairs))
    mine, row_cache_length, _ = lax.optimization_barrier((mine, row_cache_length, paired))
    steps_ab = lax.all_to_all(mine, "dp", 0, 0, tiled=True)
    base_parts = [paired[0]] + [
        lax.ppermute(paired[k], "mp", along_y(k)) for k in range(1, n_chips)
    ]

    blocks = 4
    half = blocks // 2
    block_rows = rows_dev // blocks
    n_queries = step_count * group_size
    size = block_rows * n_queries

    def attend(offset, lengths, vmem_mib):
        by_row = lambda kind: jax.ShapeDtypeStruct((half * size, head_dim), kind)
        by_row_spec = pl.BlockSpec((size, head_dim), lambda i, _: (i, 0))
        cache_spec = pl.BlockSpec((block_rows, ctx_len, head_dim), lambda i, _: (i + offset, 0, 0))
        token_spec = lambda width: pl.BlockSpec(
            (step_count, block_rows, width), lambda i, _: (0, i + offset, 0)
        )
        f32, bf16 = jnp.float32, jnp.bfloat16
        part, weights = pl.pallas_call(
            functools.partial(cache_kernel, offset),
            grid_spec=pltpu.PrefetchScalarGridSpec(
                num_scalar_prefetch=1,
                grid=(half,),
                in_specs=[
                    token_spec(group_size * head_dim),
                    token_spec(head_dim),
                    cache_spec,
                    cache_spec,
                ],
                out_specs=[by_row_spec, by_row_spec],
                scratch_shapes=[
                    pltpu.VMEM((size, head_dim), kind) for kind in (f32, bf16, f32, f32, bf16)
                ],
            ),
            out_shape=[by_row(f32), by_row(bf16)],
            compiler_params=pltpu.CompilerParams(vmem_limit_bytes=vmem_mib * 1024 * 1024),
            cost_estimate=pl.CostEstimate(
                flops=2 * 2 * half * size * 2 * ctx_len * head_dim,
                bytes_accessed=5 * 1024 * 1024,
                transcendentals=2 * half * size * head_dim,
            ),
        )(lengths, queries, rotated_token_keys, stored_key_cache[:, 0], stored_value_cache[:, 0])
        return part.reshape(half, size, head_dim), weights.reshape(half, size, head_dim)

    first_half = attend(0, row_cache_length, 60)
    steps_ab, first_half = lax.optimization_barrier((steps_ab, first_half))

    inner, new_b = pl.pallas_call(
        inner_kernel,
        out_shape=[
            jax.ShapeDtypeStruct((rank, tokens), jnp.float32),
            jax.ShapeDtypeStruct((rank, head_dim), jnp.float32),
        ],
        compiler_params=small_vmem,
        cost_estimate=pl.CostEstimate(flops=0, bytes_accessed=0, transcendentals=0),
    )(adapter_down_factor, adapter_up_factor.T, steps_ab, flat_hidden)
    inner = inner + lax.ppermute(inner, "mp", core_pairs)
    inner, base_parts = lax.optimization_barrier((inner, base_parts))
    inner, row_cache_length = lax.optimization_barrier((inner, row_cache_length))
    second_half = attend(half, row_cache_length, 52)
    inner_parts = [inner] + [lax.ppermute(inner, "mp", along_y(k)) for k in range(1, n_chips)]

    operands = [*base_parts, *inner_parts, new_b, *first_half, *second_half]
    return pl.pallas_call(
        finish_kernel,
        out_shape=jax.ShapeDtypeStruct(queries.shape, jnp.bfloat16),
        in_specs=[pl.BlockSpec(memory_space=pltpu.VMEM)] * len(operands),
        out_specs=pl.BlockSpec(memory_space=pl.ANY),
        scratch_shapes=[
            pltpu.VMEM((blocks, step_count * block_rows, head_dim), jnp.bfloat16),
            pltpu.VMEM(queries.shape, jnp.bfloat16),
            pltpu.SemaphoreType.DMA((step_count,)),
        ],
        compiler_params=small_vmem,
    )(*operands)


def solution(mesh):
    placed = (
        P(None, "dp", "mp"),
        P(None, "dp", "mp"),
        P(None, "dp", "mp"),
        P("dp", "mp", None, None),
        P("dp", "mp", None, None),
        P("dp"),
        P("mp", None),
        P(None, "mp"),
        P("dp", None, "mp"),
        P("mp", None),
        P("dp", "mp", None),
    )
    return jax.shard_map(
        shards, mesh=mesh, in_specs=placed, out_specs=P(None, "dp", "mp"), check_vma=False
    )
```

```python
import functools

import jax
import jax.numpy as jnp
from jax import lax
from jax.experimental import pallas as pl
from jax.experimental.pallas import tpu as pltpu
from jax.sharding import PartitionSpec as P

LEARNING_RATE = 0.5
ADAPTER_SCALE = 0.5


def split_bf16(x):
    high = x.astype(jnp.bfloat16)
    low = (x - high.astype(jnp.float32)).astype(jnp.bfloat16)
    return high, low


def project_kernel(place_ref, hidden_ref, weight_ref, keep_ref, send_ref):
    dim = keep_ref.shape[2]
    both = jnp.dot(hidden_ref[...], weight_ref[...], preferred_element_type=jnp.float32)
    first, second = both[:, :dim], both[:, dim:]
    odd = place_ref[1] == 1
    keep_ref[0] = jnp.where(odd, second, first)
    send_ref[0] = jnp.where(odd, first, second)


def terms_kernel(a_ref, b_ref, out_ref):
    width = a_ref.shape[1]
    slices, depth = out_ref.shape[:2]
    a = -LEARNING_RATE * a_ref[...].astype(jnp.float32)
    b = -LEARNING_RATE * b_ref[...].astype(jnp.float32)
    for i in range(slices):
        at = slice(i * depth, (i + 1) * depth)
        out_ref[i, :, :width] = a[at]
        out_ref[i, :, width:] = b[at]


def sum_kernel(in_ref, out_ref):
    total = jnp.sum(in_ref[...], axis=0, keepdims=True)
    out_ref[...] = jnp.broadcast_to(total, out_ref.shape)


def inner_kernel(a_ref, b_ref, step_ref, hidden_ref, inner_ref, new_b_ref):
    rank, width = a_ref.shape
    steps = jnp.concatenate([step_ref[i] for i in range(step_ref.shape[0])], axis=0)
    new_b_ref[...] = b_ref[...] + steps[:, width:]
    new_a = a_ref[...] + steps[:, :width]
    parts = jnp.concatenate(split_bf16(new_a), axis=0)
    both = lax.dot_general(
        hidden_ref[...], parts, (((1,), (1,)), ((), ())), preferred_element_type=jnp.float32
    )
    both = both.T
    inner_ref[...] = both[:rank] + both[rank:]


def add_kernel(keep_ref, received_ref, *out_refs):
    for k, out_ref in enumerate(out_refs):
        out_ref[...] = keep_ref[k] + received_ref[k]


def cache_kernel(
    offset, length_ref, query_ref, fresh_ref, key_ref, value_ref, part_ref, weight_ref, *scratch
):
    rows_ref, pair_ref, old_ref, new_ref, old_weight_ref = scratch
    steps, rows, width = query_ref.shape
    first = (pl.program_id(0) + offset) * rows
    ctx, dim = key_ref.shape[1:]
    heads = width // dim
    n_queries = steps * heads
    scale = 1.0 / (dim**0.5)
    for t in range(steps):
        for g in range(heads):
            at = (t * heads + g) * rows
            rows_ref[at : at + rows] = query_ref[t, :, g * dim : (g + 1) * dim].astype(jnp.float32)
    pairs = rows // 2
    lanes = 2 * ctx
    for r in range(rows):
        row = rows_ref[pl.ds(r, n_queries, stride=rows), :]
        pair_ref[r * n_queries : (r + 1) * n_queries] = row.astype(jnp.bfloat16)
    by_lane = (((1,), (1,)), ((), ()))
    mm = functools.partial(
        lax.dot_general, dimension_numbers=by_lane, preferred_element_type=jnp.float32
    )
    fresh_keys = fresh_ref[...].reshape(steps * rows, dim)
    both = 2 * n_queries
    for p in range(pairs):
        at = slice(p * both, (p + 1) * both)
        keys = key_ref[2 * p : 2 * p + 2].reshape(lanes, dim)
        old_ref[at] = mm(pair_ref[at], keys)
        new_ref[at] = mm(pair_ref[at], fresh_keys)

    lane = lax.broadcasted_iota(jnp.int32, (n_queries, lanes), 1)
    step_of = lax.broadcasted_iota(jnp.int32, (n_queries, lanes), 0) // heads
    row_of, reached = lane % rows, lane // rows <= step_of
    for r in range(rows):
        half = r % 2
        at = slice(r * n_queries, (r + 1) * n_queries)
        live = (lane >= half * ctx) & (lane < half * ctx + length_ref[first + r])
        causal = (row_of == r) & reached
        old = jnp.where(live, old_ref[at] * scale, -jnp.inf)
        new = jnp.where(causal, new_ref[at] * scale, -jnp.inf)
        top = jnp.max(jnp.maximum(old, new), axis=1, keepdims=True)
        old, new = jnp.exp(old - top), jnp.exp(new - top)
        inverse = 1.0 / jnp.sum(old + new, axis=1, keepdims=True)
        old_weight_ref[at] = (old * inverse).astype(jnp.bfloat16)
        new_ref[at] = new * inverse

    for p in range(pairs):
        at = slice(p * both, (p + 1) * both)
        values = value_ref[2 * p : 2 * p + 2].reshape(lanes, dim)
        old_ref[at] = jnp.dot(old_weight_ref[at], values, preferred_element_type=jnp.float32)
    for q in range(n_queries):
        at = slice(q * rows, (q + 1) * rows)
        query = pl.ds(q, rows, stride=n_queries)
        part_ref[at] = old_ref[query, :]
        weight_ref[at] = new_ref[query, :].astype(jnp.bfloat16)


def finish_kernel(v0, v1, v2, v3, u0, u1, u2, u3, b_ref, *refs):
    *halves, out_ref, value_ref, held_ref, sems = refs
    blocks, lanes, dim = value_ref.shape
    steps, rows, width = held_ref.shape
    block_rows = rows // blocks
    heads = width // dim
    u = (u0[...] + u1[...]) + (u2[...] + u3[...])
    u_high, u_low = split_bf16(u)
    b_high, b_low = split_bf16(b_ref[...])
    dims = (((0,), (0,)), ((), ()))
    mm = functools.partial(
        lax.dot_general, dimension_numbers=dims, preferred_element_type=jnp.float32
    )
    delta = mm(u_high, b_high) + (mm(u_low, b_high) + mm(u_high, b_low))
    values = (v0[...] + v1[...]) + (v2[...] + v3[...]) + ADAPTER_SCALE * delta
    values = values.astype(jnp.bfloat16)
    for i in range(blocks):
        for s in range(steps):
            at = s * rows + i * block_rows
            value_ref[i, s * block_rows : (s + 1) * block_rows] = values[at : at + block_rows]

    size = heads * block_rows
    half = blocks // 2

    def written(t):
        return pltpu.make_async_copy(held_ref.at[t], out_ref.at[t], sems.at[t])

    def one_step(t, carry):
        at = pl.ds(pl.multiple_of(t * size, size), size)
        for i in range(blocks):
            part_ref, weight_ref = halves[2 * (i // half) : 2 * (i // half) + 2]
            fresh = jnp.dot(
                weight_ref[i % half, at, :], value_ref[i], preferred_element_type=jnp.float32
            )
            context = part_ref[i % half, at, :] + fresh
            for g in range(heads):
                held_ref[t, i * block_rows : (i + 1) * block_rows, g * dim : (g + 1) * dim] = (
                    context[g * block_rows : (g + 1) * block_rows].astype(held_ref.dtype)
                )
        written(t).start()
        return carry

    lax.fori_loop(0, steps, one_step, 0)
    for t in range(steps):
        written(t).wait()


def shards(
    hidden,
    queries,
    rotated_token_keys,
    stored_key_cache,
    stored_value_cache,
    row_cache_length,
    value_weight_matrix,
    adapter_down_factor,
    learner_down_gradient,
    adapter_up_factor,
    learner_up_gradient,
):
    step_count, rows_dev, width_dev = hidden.shape
    heads_dev, ctx_len, head_dim = stored_key_cache.shape[1:]
    group_size = queries.shape[2] // (heads_dev * head_dim)
    rank = adapter_down_factor.shape[0]
    n_dp = lax.axis_size("dp")
    n_mp = lax.axis_size("mp")
    tokens = step_count * rows_dev
    flat_hidden = hidden.reshape(tokens, width_dev)

    small_vmem = pltpu.CompilerParams(vmem_limit_bytes=16 * 1024 * 1024)

    slices = jax.ShapeDtypeStruct((n_dp, rank // n_dp, width_dev + head_dim), jnp.float32)
    terms = pl.pallas_call(
        terms_kernel,
        out_shape=slices,
        compiler_params=pltpu.CompilerParams(vmem_limit_bytes=60 * 1024 * 1024),
    )(
        learner_down_gradient[0], learner_up_gradient[0].T
    )
    mine = lax.all_to_all(terms, "dp", 0, 0, tiled=True)
    mine = pl.pallas_call(sum_kernel, out_shape=slices, compiler_params=small_vmem)(mine)

    n_chips = n_mp // 2
    here = lax.axis_index("mp")
    place = jnp.stack([here // 2, here % 2]).astype(jnp.int32)
    chunk = jax.ShapeDtypeStruct((n_chips, tokens, head_dim), jnp.float32)
    chunk_spec = pl.BlockSpec((1, tokens, head_dim), lambda k, place: (k, 0, 0))
    keep, send = pl.pallas_call(
        project_kernel,
        grid_spec=pltpu.PrefetchScalarGridSpec(
            num_scalar_prefetch=1,
            grid=(n_chips,),
            in_specs=[
                pl.BlockSpec((tokens, width_dev), lambda k, place: (0, 0)),
                pl.BlockSpec(
                    (width_dev, 2 * head_dim), lambda k, place: (0, lax.rem(place[0] + k, n_chips))
                ),
            ],
            out_specs=[chunk_spec, chunk_spec],
        ),
        out_shape=[chunk, chunk],
        compiler_params=small_vmem,
        cost_estimate=pl.CostEstimate(
            flops=2 * tokens * width_dev * value_weight_matrix.shape[1],
            bytes_accessed=10 * 1024 * 1024,
            transcendentals=0,
        ),
    )(place, flat_hidden, value_weight_matrix)
    core_pairs = [(i, i ^ 1) for i in range(n_mp)]
    along_y = lambda k: [(i, (i + 2 * k) % n_mp) for i in range(n_mp)]
    paired = pl.pallas_call(
        add_kernel,
        out_shape=[jax.ShapeDtypeStruct((tokens, head_dim), jnp.float32)] * n_chips,
        compiler_params=small_vmem,
    )(keep, lax.ppermute(send, "mp", core_pairs))
    mine, row_cache_length, _ = lax.optimization_barrier((mine, row_cache_length, paired))
    steps_ab = lax.all_to_all(mine, "dp", 0, 0, tiled=True)
    base_parts = [paired[0]] + [
        lax.ppermute(paired[k], "mp", along_y(k)) for k in range(1, n_chips)
    ]

    blocks = 4
    half = blocks // 2
    block_rows = rows_dev // blocks
    n_queries = step_count * group_size
    size = block_rows * n_queries

    def attend(offset, lengths, vmem_mib):
        by_row = lambda kind: jax.ShapeDtypeStruct((half * size, head_dim), kind)
        by_row_spec = pl.BlockSpec((size, head_dim), lambda i, _: (i, 0))
        cache_spec = pl.BlockSpec((block_rows, ctx_len, head_dim), lambda i, _: (i + offset, 0, 0))
        token_spec = lambda width: pl.BlockSpec(
            (step_count, block_rows, width), lambda i, _: (0, i + offset, 0)
        )
        f32, bf16 = jnp.float32, jnp.bfloat16
        part, weights = pl.pallas_call(
            functools.partial(cache_kernel, offset),
            grid_spec=pltpu.PrefetchScalarGridSpec(
                num_scalar_prefetch=1,
                grid=(half,),
                in_specs=[
                    token_spec(group_size * head_dim),
                    token_spec(head_dim),
                    cache_spec,
                    cache_spec,
                ],
                out_specs=[by_row_spec, by_row_spec],
                scratch_shapes=[
                    pltpu.VMEM((size, head_dim), kind) for kind in (f32, bf16, f32, f32, bf16)
                ],
            ),
            out_shape=[by_row(f32), by_row(bf16)],
            compiler_params=pltpu.CompilerParams(vmem_limit_bytes=vmem_mib * 1024 * 1024),
            cost_estimate=pl.CostEstimate(
                flops=2 * 2 * half * size * 2 * ctx_len * head_dim,
                bytes_accessed=5 * 1024 * 1024,
                transcendentals=2 * half * size * head_dim,
            ),
        )(lengths, queries, rotated_token_keys, stored_key_cache[:, 0], stored_value_cache[:, 0])
        return part.reshape(half, size, head_dim), weights.reshape(half, size, head_dim)

    first_half = attend(0, row_cache_length, 60)
    steps_ab, first_half = lax.optimization_barrier((steps_ab, first_half))

    inner, new_b = pl.pallas_call(
        inner_kernel,
        out_shape=[
            jax.ShapeDtypeStruct((rank, tokens), jnp.float32),
            jax.ShapeDtypeStruct((rank, head_dim), jnp.float32),
        ],
        compiler_params=small_vmem,
        cost_estimate=pl.CostEstimate(flops=0, bytes_accessed=0, transcendentals=0),
    )(adapter_down_factor, adapter_up_factor.T, steps_ab, flat_hidden)
    inner = inner + lax.ppermute(inner, "mp", core_pairs)
    inner, base_parts = lax.optimization_barrier((inner, base_parts))
    inner, row_cache_length = lax.optimization_barrier((inner, row_cache_length))
    second_half = attend(half, row_cache_length, 52)
    distances = sorted(range(1, n_chips), key=lambda k: min(k, n_chips - k))
    inner_parts = [inner] + [lax.ppermute(inner, "mp", along_y(k)) for k in distances]

    operands = [*base_parts, *inner_parts, new_b, *first_half, *second_half]
    return pl.pallas_call(
        finish_kernel,
        out_shape=jax.ShapeDtypeStruct(queries.shape, jnp.bfloat16),
        in_specs=[pl.BlockSpec(memory_space=pltpu.VMEM)] * len(operands),
        out_specs=pl.BlockSpec(memory_space=pl.ANY),
        scratch_shapes=[
            pltpu.VMEM((blocks, step_count * block_rows, head_dim), jnp.bfloat16),
            pltpu.VMEM(queries.shape, jnp.bfloat16),
            pltpu.SemaphoreType.DMA((step_count,)),
        ],
        compiler_params=small_vmem,
    )(*operands)


def solution(mesh):
    placed = (
        P(None, "dp", "mp"),
        P(None, "dp", "mp"),
        P(None, "dp", "mp"),
        P("dp", "mp", None, None),
        P("dp", "mp", None, None),
        P("dp"),
        P("mp", None),
        P(None, "mp"),
        P("dp", None, "mp"),
        P("mp", None),
        P("dp", "mp", None),
    )
    return jax.shard_map(
        shards, mesh=mesh, in_specs=placed, out_specs=P(None, "dp", "mp"), check_vma=False
    )
```

```python
import functools

import jax
import jax.numpy as jnp
from jax import lax
from jax.experimental import pallas as pl
from jax.experimental.pallas import tpu as pltpu
from jax.sharding import PartitionSpec as P

LEARNING_RATE = 0.5
ADAPTER_SCALE = 0.5


def split_bf16(x):
    high = x.astype(jnp.bfloat16)
    low = (x - high.astype(jnp.float32)).astype(jnp.bfloat16)
    return high, low


def project_kernel(place_ref, hidden_ref, weight_ref, keep_ref, send_ref):
    dim = keep_ref.shape[2]
    both = jnp.dot(hidden_ref[...], weight_ref[...], preferred_element_type=jnp.float32)
    first, second = both[:, :dim], both[:, dim:]
    odd = place_ref[1] == 1
    keep_ref[0] = jnp.where(odd, second, first)
    send_ref[0] = jnp.where(odd, first, second)


def terms_kernel(a_ref, b_ref, out_ref):
    width = a_ref.shape[1]
    slices, depth = out_ref.shape[:2]
    a = -LEARNING_RATE * a_ref[...].astype(jnp.float32)
    b = -LEARNING_RATE * b_ref[...].astype(jnp.float32)
    for i in range(slices):
        at = slice(i * depth, (i + 1) * depth)
        out_ref[i, :, :width] = a[at]
        out_ref[i, :, width:] = b[at]


def sum_kernel(in_ref, out_ref):
    total = jnp.sum(in_ref[...], axis=0, keepdims=True)
    out_ref[...] = jnp.broadcast_to(total, out_ref.shape)


def inner_kernel(a_ref, b_ref, step_ref, hidden_ref, inner_ref, new_b_ref):
    rank, width = a_ref.shape
    steps = jnp.concatenate([step_ref[i] for i in range(step_ref.shape[0])], axis=0)
    new_b_ref[...] = b_ref[...] + steps[:, width:]
    new_a = a_ref[...] + steps[:, :width]
    parts = jnp.concatenate(split_bf16(new_a), axis=0)
    both = lax.dot_general(
        hidden_ref[...], parts, (((1,), (1,)), ((), ())), preferred_element_type=jnp.float32
    )
    both = both.T
    inner_ref[...] = both[:rank] + both[rank:]


def add_kernel(keep_ref, received_ref, *out_refs):
    for k, out_ref in enumerate(out_refs):
        out_ref[...] = keep_ref[k] + received_ref[k]


def cache_kernel(
    offset, length_ref, query_ref, fresh_ref, key_ref, value_ref, part_ref, weight_ref, *scratch
):
    rows_ref, pair_ref, old_ref, new_ref, old_weight_ref = scratch
    steps, rows, width = query_ref.shape
    first = (pl.program_id(0) + offset) * rows
    ctx, dim = key_ref.shape[1:]
    heads = width // dim
    n_queries = steps * heads
    scale = 1.0 / (dim**0.5)
    for t in range(steps):
        for g in range(heads):
            at = (t * heads + g) * rows
            rows_ref[at : at + rows] = query_ref[t, :, g * dim : (g + 1) * dim].astype(jnp.float32)
    pairs = rows // 2
    lanes = 2 * ctx
    for r in range(rows):
        row = rows_ref[pl.ds(r, n_queries, stride=rows), :]
        pair_ref[r * n_queries : (r + 1) * n_queries] = row.astype(jnp.bfloat16)
    by_lane = (((1,), (1,)), ((), ()))
    mm = functools.partial(
        lax.dot_general, dimension_numbers=by_lane, preferred_element_type=jnp.float32
    )
    fresh_keys = fresh_ref[...].reshape(steps * rows, dim)
    both = 2 * n_queries
    for p in range(pairs):
        at = slice(p * both, (p + 1) * both)
        keys = key_ref[2 * p : 2 * p + 2].reshape(lanes, dim)
        old_ref[at] = mm(pair_ref[at], keys)
        new_ref[at] = mm(pair_ref[at], fresh_keys)

    lane = lax.broadcasted_iota(jnp.int32, (n_queries, lanes), 1)
    step_of = lax.broadcasted_iota(jnp.int32, (n_queries, lanes), 0) // heads
    row_of, reached = lane % rows, lane // rows <= step_of
    for r in range(rows):
        half = r % 2
        at = slice(r * n_queries, (r + 1) * n_queries)
        live = (lane >= half * ctx) & (lane < half * ctx + length_ref[first + r])
        causal = (row_of == r) & reached
        old = jnp.where(live, old_ref[at] * scale, -jnp.inf)
        new = jnp.where(causal, new_ref[at] * scale, -jnp.inf)
        top = jnp.max(jnp.maximum(old, new), axis=1, keepdims=True)
        old, new = jnp.exp(old - top), jnp.exp(new - top)
        inverse = 1.0 / jnp.sum(old + new, axis=1, keepdims=True)
        old_weight_ref[at] = (old * inverse).astype(jnp.bfloat16)
        new_ref[at] = new * inverse

    for p in range(pairs):
        at = slice(p * both, (p + 1) * both)
        values = value_ref[2 * p : 2 * p + 2].reshape(lanes, dim)
        old_ref[at] = jnp.dot(old_weight_ref[at], values, preferred_element_type=jnp.float32)
    for q in range(n_queries):
        at = slice(q * rows, (q + 1) * rows)
        query = pl.ds(q, rows, stride=n_queries)
        part_ref[at] = old_ref[query, :]
        weight_ref[at] = new_ref[query, :].astype(jnp.bfloat16)


def finish_kernel(v0, v1, v2, v3, u0, u1, u2, u3, b_ref, *refs):
    *parts, out_ref, value_ref, held_ref, sems = refs
    blocks, lanes, dim = value_ref.shape
    steps, rows, width = held_ref.shape
    block_rows = rows // blocks
    heads = width // dim
    u = (u0[...] + u1[...]) + (u2[...] + u3[...])
    u_high, u_low = split_bf16(u)
    b_high, b_low = split_bf16(b_ref[...])
    dims = (((0,), (0,)), ((), ()))
    mm = functools.partial(
        lax.dot_general, dimension_numbers=dims, preferred_element_type=jnp.float32
    )
    delta = mm(u_high, b_high) + (mm(u_low, b_high) + mm(u_high, b_low))
    values = (v0[...] + v1[...]) + (v2[...] + v3[...]) + ADAPTER_SCALE * delta
    values = values.astype(jnp.bfloat16)
    for i in range(blocks):
        for s in range(steps):
            at = s * rows + i * block_rows
            value_ref[i, s * block_rows : (s + 1) * block_rows] = values[at : at + block_rows]

    size = heads * block_rows
    split = parts[0].shape[0]
    copies = []
    for t in range(steps):
        at = slice(t * size, (t + 1) * size)
        for i in range(blocks):
            part_ref, weight_ref = parts[:2] if i < split else parts[2:]
            k = i if i < split else i - split
            fresh = jnp.dot(
                weight_ref[k, at], value_ref[i], preferred_element_type=jnp.float32
            )
            context = part_ref[k, at] + fresh
            for g in range(heads):
                held_ref[t, i * block_rows : (i + 1) * block_rows, g * dim : (g + 1) * dim] = (
                    context[g * block_rows : (g + 1) * block_rows].astype(held_ref.dtype)
                )
        copies.append(pltpu.make_async_copy(held_ref.at[t], out_ref.at[t], sems.at[t]))
        copies[-1].start()
    for copy in copies:
        copy.wait()


def shards(
    hidden,
    queries,
    rotated_token_keys,
    stored_key_cache,
    stored_value_cache,
    row_cache_length,
    value_weight_matrix,
    adapter_down_factor,
    learner_down_gradient,
    adapter_up_factor,
    learner_up_gradient,
):
    step_count, rows_dev, width_dev = hidden.shape
    heads_dev, ctx_len, head_dim = stored_key_cache.shape[1:]
    group_size = queries.shape[2] // (heads_dev * head_dim)
    rank = adapter_down_factor.shape[0]
    n_dp = lax.axis_size("dp")
    n_mp = lax.axis_size("mp")
    tokens = step_count * rows_dev
    flat_hidden = hidden.reshape(tokens, width_dev)

    small_vmem = pltpu.CompilerParams(vmem_limit_bytes=16 * 1024 * 1024)

    slices = jax.ShapeDtypeStruct((n_dp, rank // n_dp, width_dev + head_dim), jnp.float32)
    terms = pl.pallas_call(
        terms_kernel,
        out_shape=slices,
        compiler_params=pltpu.CompilerParams(vmem_limit_bytes=60 * 1024 * 1024),
    )(
        learner_down_gradient[0], learner_up_gradient[0].T
    )
    mine = lax.all_to_all(terms, "dp", 0, 0, tiled=True)
    mine = pl.pallas_call(sum_kernel, out_shape=slices, compiler_params=small_vmem)(mine)

    n_chips = n_mp // 2
    here = lax.axis_index("mp")
    place = jnp.stack([here // 2, here % 2]).astype(jnp.int32)
    chunk = jax.ShapeDtypeStruct((n_chips, tokens, head_dim), jnp.float32)
    chunk_spec = pl.BlockSpec((1, tokens, head_dim), lambda k, place: (k, 0, 0))
    keep, send = pl.pallas_call(
        project_kernel,
        grid_spec=pltpu.PrefetchScalarGridSpec(
            num_scalar_prefetch=1,
            grid=(n_chips,),
            in_specs=[
                pl.BlockSpec((tokens, width_dev), lambda k, place: (0, 0)),
                pl.BlockSpec(
                    (width_dev, 2 * head_dim), lambda k, place: (0, lax.rem(place[0] + k, n_chips))
                ),
            ],
            out_specs=[chunk_spec, chunk_spec],
        ),
        out_shape=[chunk, chunk],
        compiler_params=small_vmem,
        cost_estimate=pl.CostEstimate(
            flops=2 * tokens * width_dev * value_weight_matrix.shape[1],
            bytes_accessed=10 * 1024 * 1024,
            transcendentals=0,
        ),
    )(place, flat_hidden, value_weight_matrix)
    core_pairs = [(i, i ^ 1) for i in range(n_mp)]
    along_y = lambda k: [(i, (i + 2 * k) % n_mp) for i in range(n_mp)]
    paired = pl.pallas_call(
        add_kernel,
        out_shape=[jax.ShapeDtypeStruct((tokens, head_dim), jnp.float32)] * n_chips,
        compiler_params=small_vmem,
    )(keep, lax.ppermute(send, "mp", core_pairs))
    mine, row_cache_length, _ = lax.optimization_barrier((mine, row_cache_length, paired))
    steps_ab = lax.all_to_all(mine, "dp", 0, 0, tiled=True)
    base_parts = [paired[0]] + [
        lax.ppermute(paired[k], "mp", along_y(k)) for k in range(1, n_chips)
    ]

    blocks = 4
    early_blocks = 3
    block_rows = rows_dev // blocks
    n_queries = step_count * group_size
    size = block_rows * n_queries

    def attend(offset, count, lengths, vmem_mib):
        by_row = lambda kind: jax.ShapeDtypeStruct((count * size, head_dim), kind)
        by_row_spec = pl.BlockSpec((size, head_dim), lambda i, _: (i, 0))
        cache_spec = pl.BlockSpec((block_rows, ctx_len, head_dim), lambda i, _: (i + offset, 0, 0))
        token_spec = lambda width: pl.BlockSpec(
            (step_count, block_rows, width), lambda i, _: (0, i + offset, 0)
        )
        f32, bf16 = jnp.float32, jnp.bfloat16
        part, weights = pl.pallas_call(
            functools.partial(cache_kernel, offset),
            grid_spec=pltpu.PrefetchScalarGridSpec(
                num_scalar_prefetch=1,
                grid=(count,),
                in_specs=[
                    token_spec(group_size * head_dim),
                    token_spec(head_dim),
                    cache_spec,
                    cache_spec,
                ],
                out_specs=[by_row_spec, by_row_spec],
                scratch_shapes=[
                    pltpu.VMEM((size, head_dim), kind) for kind in (f32, bf16, f32, f32, bf16)
                ],
            ),
            out_shape=[by_row(f32), by_row(bf16)],
            compiler_params=pltpu.CompilerParams(vmem_limit_bytes=vmem_mib * 1024 * 1024),
            cost_estimate=pl.CostEstimate(
                flops=2 * 2 * count * size * 2 * ctx_len * head_dim,
                bytes_accessed=5 * 1024 * 1024,
                transcendentals=2 * count * size * head_dim,
            ),
        )(lengths, queries, rotated_token_keys, stored_key_cache[:, 0], stored_value_cache[:, 0])
        return part.reshape(count, size, head_dim), weights.reshape(count, size, head_dim)

    first_part = attend(0, early_blocks, row_cache_length, 60)
    steps_ab, first_part = lax.optimization_barrier((steps_ab, first_part))

    inner, new_b = pl.pallas_call(
        inner_kernel,
        out_shape=[
            jax.ShapeDtypeStruct((rank, tokens), jnp.float32),
            jax.ShapeDtypeStruct((rank, head_dim), jnp.float32),
        ],
        compiler_params=small_vmem,
        cost_estimate=pl.CostEstimate(flops=0, bytes_accessed=0, transcendentals=0),
    )(adapter_down_factor, adapter_up_factor.T, steps_ab, flat_hidden)
    inner = inner + lax.ppermute(inner, "mp", core_pairs)
    inner, base_parts = lax.optimization_barrier((inner, base_parts))
    inner, row_cache_length = lax.optimization_barrier((inner, row_cache_length))
    second_part = attend(early_blocks, blocks - early_blocks, row_cache_length, 53)
    distances = sorted(range(1, n_chips), key=lambda k: min(k, n_chips - k))
    inner_parts = [inner] + [lax.ppermute(inner, "mp", along_y(k)) for k in distances]

    operands = [*base_parts, *inner_parts, new_b, *first_part, *second_part]
    return pl.pallas_call(
        finish_kernel,
        out_shape=jax.ShapeDtypeStruct(queries.shape, jnp.bfloat16),
        in_specs=[pl.BlockSpec(memory_space=pltpu.VMEM)] * len(operands),
        out_specs=pl.BlockSpec(memory_space=pl.ANY),
        scratch_shapes=[
            pltpu.VMEM((blocks, step_count * block_rows, head_dim), jnp.bfloat16),
            pltpu.VMEM(queries.shape, jnp.bfloat16),
            pltpu.SemaphoreType.DMA((step_count,)),
        ],
        compiler_params=small_vmem,
    )(*operands)


def solution(mesh):
    placed = (
        P(None, "dp", "mp"),
        P(None, "dp", "mp"),
        P(None, "dp", "mp"),
        P("dp", "mp", None, None),
        P("dp", "mp", None, None),
        P("dp"),
        P("mp", None),
        P(None, "mp"),
        P("dp", None, "mp"),
        P("mp", None),
        P("dp", "mp", None),
    )
    return jax.shard_map(
        shards, mesh=mesh, in_specs=placed, out_specs=P(None, "dp", "mp"), check_vma=False
    )
```
